32 devices in a mesh: state: 4 (over y, core), walker: 8 (over z, x).
Axes of the slice: x: 2, y: 2, z: 4, core: 2. Of those that a mesh axis runs over, the one named last changes fastest.
Arguments:
- walkers: float32 [8, 8, 126], P('state', 'walker'), may hold values from -8 to 8
- nuclei: float32 [12, 3], replicated, may hold values from -5 to 5
- w_embed: float32 [8, 48, 256], P('state'), may hold values from -0.875 to 0.875
- w_query: float32 [8, 1, 256, 256], P('state'), may hold values from -16 to 16
- w_key: float32 [8, 1, 256, 256], P('state'), may hold values from -0.375 to 0.375
- w_value: float32 [8, 1, 256, 256], P('state'), may hold values from -0.375 to 0.375
- w_attn_out: float32 [8, 1, 256, 256], P('state'), may hold values from -0.375 to 0.375
- w_mlp: float32 [8, 1, 256, 256], P('state'), may hold values from -0.375 to 0.375
- b_mlp: float32 [8, 1, 256], P('state'), may hold values from -3 to 3
- w_out: float32 [8, 256], P('state'), may hold values from -0.375 to 0.375
Outputs:
- margins: float32 [8, 8], replicated
- grad_embed: float32 [8, 48, 256], P('state')
- grad_query: float32 [8, 1, 256, 256], P('state')
- grad_key: float32 [8, 1, 256, 256], P('state')
- grad_value: float32 [8, 1, 256, 256], P('state')
- grad_attn_out: float32 [8, 1, 256, 256], P('state')
- grad_mlp: float32 [8, 1, 256, 256], P('state')
- grad_bias: float32 [8, 1, 256], P('state')
- grad_out: float32 [8, 256], P('state')
The draws below stay inside these ranges and needn't reach their ends.
All inputs are finite; a program needn't handle non-finite values.
Results may differ from the reference program's by a relative error of at most 0.0003.
Values sent between devices are 32-bit elements; how exact they have to be, the bound alone decides.
A program may use at most 64 MiB of HBM per device.

```python
import math
import jax
import jax.numpy as jnp
from jax import lax

D = 256
HEADS = 4
NE = 42
NA = 12
FEAT = 48
LAYERS = 1
NSTATES = 8
WALKERS = 8


def draw_w_query(key, part):
    base = jax.random.truncated_normal(key, -4.0, 4.0, (NSTATES, LAYERS, D, D), jnp.float32)
    return base * (16.0 / D)


def block_levels(rng, shape, shards, least, largest):
    loudness = 1.0
    for dim, blocks in shards:
        draws = jax.random.uniform(jax.random.fold_in(jax.random.fold_in(rng, 6), dim), (blocks,), jnp.float32, least / len(shards), largest / len(shards))
        loudness = loudness * jnp.repeat(jnp.exp(draws), shape[dim] // blocks).reshape((-1,) + (1,) * (len(shape) - 1 - dim))
    return loudness


def scatter_about(own_key, extent, deviation, limit, split=(), kind=jnp.bfloat16):
    entries = jax.random.normal(own_key, extent, jnp.float32) * deviation
    if len(split) > 0:
        entries = block_levels(own_key, extent, split, -0.22, 0.18) * entries
    return jnp.clip(entries, min=-limit, max=limit).astype(kind)


def setup_inputs(seed: int = 0) -> dict:
    key_list = jax.random.split(jax.random.key(seed), 11)
    return {
        "walkers": scatter_about(key_list[0], (NSTATES, WALKERS, 3 * NE), 1.5, 8.0, ((0, 4), (1, 8)), jnp.float32),
        "nuclei": scatter_about(key_list[1], (NA, 3), 1.3, 5.0, (), jnp.float32),
        "w_embed": scatter_about(key_list[2], (NSTATES, FEAT, D), FEAT ** -0.5, 0.875, ((0, 4),), jnp.float32),
        "w_query": draw_w_query(jax.random.fold_in(key_list[10], 71), 0),
        "w_key": scatter_about(key_list[4], (NSTATES, LAYERS, D, D), D ** -0.5, 0.375, ((0, 4),), jnp.float32),
        "w_value": scatter_about(key_list[5], (NSTATES, LAYERS, D, D), D ** -0.5, 0.375, ((0, 4),), jnp.float32),
        "w_attn_out": scatter_about(key_list[6], (NSTATES, LAYERS, D, D), D ** -0.5, 0.375, ((0, 4),), jnp.float32),
        "w_mlp": scatter_about(key_list[7], (NSTATES, LAYERS, D, D), D ** -0.5, 0.375, ((0, 4),), jnp.float32),
        "b_mlp": scatter_about(key_list[8], (NSTATES, LAYERS, D), 0.5, 3.0, ((0, 4),), jnp.float32),
        "w_out": scatter_about(key_list[9], (NSTATES, D), D ** -0.5, 0.375, ((0, 4),), jnp.float32),
    }


highest = lax.Precision.HIGHEST
eps = 1e-05

def layer_norm(hidden):
    centre = hidden - lax.optimization_barrier(jnp.mean(hidden, axis=-1, keepdims=True))
    spread = lax.optimization_barrier(jnp.mean(centre * centre, axis=-1, keepdims=True))
    return centre / jnp.sqrt(spread + eps)

def electron_features(positions, nuclei):
    batch_size = positions.shape[0]
    electrons = positions.reshape(batch_size, -1, 1, 3)
    offset = electrons - nuclei[None, None, :, :]
    distance = jnp.sqrt(lax.optimization_barrier(jnp.sum(offset * offset, axis=-1, keepdims=True)) + 1.0)
    joined = jnp.concatenate([offset, distance], axis=-1)
    return joined.reshape(batch_size, electrons.shape[1], -1)

def network(parameters, electron_feats):
    w_embed, w_query, w_key, w_value, w_attn_out, w_mlp, b_mlp, w_out = parameters
    batch_size, electron_count = (electron_feats.shape[0], electron_feats.shape[1])
    width = w_embed.shape[1]
    head_size = width // HEADS
    hidden = jnp.einsum('bef,fd->bed', electron_feats, w_embed, precision=highest)
    for layer_index in range(w_query.shape[0]):
        normed = layer_norm(hidden)
        queries = jnp.einsum('bed,dc->bec', normed, w_query[layer_index], precision=highest).reshape(batch_size, electron_count, HEADS, head_size)
        key_heads = jnp.einsum('bed,dc->bec', normed, w_key[layer_index], precision=highest).reshape(batch_size, electron_count, HEADS, head_size)
        value_heads = jnp.einsum('bed,dc->bec', normed, w_value[layer_index], precision=highest).reshape(batch_size, electron_count, HEADS, head_size)
        scores = jnp.einsum('behc,bfhc->bhef', queries, key_heads, precision=highest) / math.sqrt(head_size)
        row_max = lax.stop_gradient(lax.optimization_barrier(jnp.max(scores, axis=-1, keepdims=True)))
        weights = jnp.exp(scores - row_max)
        attention = weights / lax.optimization_barrier(jnp.sum(weights, axis=-1, keepdims=True))
        mixed = jnp.einsum('bhef,bfhc->behc', attention, value_heads, precision=highest).reshape(batch_size, electron_count, width)
        hidden = hidden + jnp.einsum('bed,dc->bec', mixed, w_attn_out[layer_index], precision=highest)
        inner = jnp.einsum('bed,dc->bec', layer_norm(hidden), w_mlp[layer_index], precision=highest)
        hidden = hidden + jnp.tanh(inner + b_mlp[layer_index])
    return jnp.einsum('bed,d->b', hidden, w_out, precision=highest) / electron_count

def reference(walkers, nuclei, w_embed, w_query, w_key, w_value, w_attn_out, w_mlp, b_mlp, w_out):
    state_total, walker_count = (walkers.shape[0], walkers.shape[1])
    parameters = (w_embed, w_query, w_key, w_value, w_attn_out, w_mlp, b_mlp, w_out)
    electron_feats = electron_features(walkers.reshape(state_total * walker_count, -1), nuclei)
    log_amplitude = lax.map(lambda net_params: network(net_params, electron_feats), parameters)
    log_amplitude = log_amplitude.reshape(state_total, state_total, walker_count)
    home_logs = jnp.diagonal(log_amplitude, axis1=0, axis2=1).T
    ratios = jnp.exp(log_amplitude - home_logs[None])
    margins = lax.optimization_barrier(jnp.mean(ratios, axis=2)).T
    identity = jnp.eye(state_total, dtype=jnp.float32)
    coupling = margins.T * (1.0 - identity)
    denominator = jnp.einsum('ij,jix->ix', coupling, ratios, precision=highest) / walker_count
    cotangent = coupling.T[:, :, None] * ratios / walker_count - identity[:, :, None] * denominator[None]

    def pull_back(inputs):
        net_params, net_cotangent = inputs
        _, pullback = jax.vjp(lambda chosen: network(chosen, electron_feats), net_params)
        return pullback(net_cotangent)[0]
    gradients = lax.map(pull_back, (parameters, cotangent.reshape(state_total, -1)))
    return (margins, gradients[0], gradients[1], gradients[2], gradients[3], gradients[4], gradients[5], gradients[6], gradients[7])
```

```python
import functools
import math

import jax
import jax.numpy as jnp
from jax import lax
from jax.experimental import pallas as pl
from jax.experimental.pallas import tpu as pltpu
from jax.sharding import PartitionSpec as P

HEADS = 4
EPS = 1e-05
F32 = jnp.float32
BF16 = jnp.bfloat16
MESH = pl.DeviceIdType.MESH
WALKERS_PER_BLOCK = 4

NN = (((1,), (0,)), ((), ()))
NT = (((1,), (1,)), ((), ()))
TN = (((0,), (0,)), ((), ()))


def split(x, parts):
    out = []
    for part in range(parts):
        piece = x.astype(BF16)
        out.append(piece)
        if part + 1 < parts:
            x = x - piece.astype(F32)
    return out


def product(a, b, dims, parts):
    total = None
    for order in range(parts - 1, -1, -1):
        for i in range(order + 1):
            term = lax.dot_general(a[i], b[order - i], dims, preferred_element_type=F32)
            total = term if total is None else total + term
    return total


def normalise(hidden):
    centre = hidden - jnp.mean(hidden, axis=-1, keepdims=True)
    spread = jnp.mean(centre * centre, axis=-1, keepdims=True)
    scale = 1.0 / jnp.sqrt(spread + EPS)
    return centre * scale, scale


def normalise_back(grad, normed, scale):
    mean = jnp.mean(grad, axis=-1, keepdims=True)
    along = jnp.mean(grad * normed, axis=-1, keepdims=True)
    return scale * (grad - mean - normed * along)


def kernel(
    cfg,
    walkers, nuclei, w_embed, w_query, w_key, w_value, w_attn, w_mlp, b_mlp, w_out,
    margins, o_query, o_key, o_value, o_attn, o_mlp, o_extra,
    wbuf, raw_embed, raw, vecs, s_embed, s_w, feats, x1, r1, q, k, v, att, mixed, x2, r2, act, h2,
    g1, gk, gq, gv, dm, lrow, tab, part, part_extra, rbuf, rbuf_extra, ccol,
    load_sem, walk_send, walk_recv, tab_send, tab_recv, rs_send, rs_recv, ag_send, ag_recv,
):
    S, W, L, G, N, NE, PAD, D, FEAT, CH, EC = cfg
    held = N * L
    head_size = D // HEADS
    WB = WALKERS_PER_BLOCK
    RB = WB * PAD
    blocks = held // WB
    total_walkers = W
    s = lax.axis_index("state")
    w = lax.axis_index("walker")
    j = lax.div(w, G)
    g = lax.rem(w, G)
    net = s * L + j
    me = s * W + w

    loads = [pltpu.make_async_copy(w_embed.at[j], raw_embed, load_sem.at[0])]
    for n, ref in enumerate((w_query, w_key, w_value, w_attn, w_mlp)):
        loads.append(pltpu.make_async_copy(ref.at[j, 0], raw.at[n], load_sem.at[1 + n]))
    for copy in loads:
        copy.start()

    barrier = pltpu.get_barrier_semaphore()

    def greet(d, carry):
        other = lax.rem(me + d, S * W)
        pl.semaphore_signal(
            barrier, inc=1, device_id=(lax.div(other, W), lax.rem(other, W)), device_id_type=MESH
        )
        return carry

    lax.fori_loop(1, S * W, greet, 0)

    for copy in loads:
        copy.wait()
    for i, piece in enumerate(split(raw_embed[...], 3)):
        s_embed[i] = piece
    for n in range(5):
        for i, piece in enumerate(split(raw[n], 3 if n < 2 else 2)):
            s_w[n, i] = piece
    vecs[0:1, :] = b_mlp[j]
    vecs[1:2, :] = w_out[pl.ds(j, 1), :]

    pl.semaphore_wait(barrier, S * W - 1)

    def walk_copy(s_to, j_to):
        return pltpu.make_async_remote_copy(
            src_ref=walkers,
            dst_ref=wbuf.at[s, lax.rem(w, L)],
            send_sem=walk_send.at[s_to, j_to],
            recv_sem=walk_recv.at[s, lax.rem(w, L)],
            device_id=(s_to, j_to * G + lax.div(w, L)),
            device_id_type=MESH,
        )

    def walk_arrival(s_from, x_from):
        return pltpu.make_async_remote_copy(
            src_ref=walkers,
            dst_ref=wbuf.at[s_from, x_from],
            send_sem=walk_send.at[0, 0],
            recv_sem=walk_recv.at[s_from, x_from],
            device_id=(s_from, L * g + x_from),
            device_id_type=MESH,
        )

    for s_to in range(S):
        for j_to in range(L):
            to_me = s_to * W + j_to * G + lax.div(w, L) == me

            @pl.when(jnp.logical_not(to_me))
            def _():
                walk_copy(s_to, j_to).start()

            @pl.when(to_me)
            def _():
                wbuf[s, lax.rem(w, L)] = walkers[...]

    lane = lax.broadcasted_iota(jnp.int32, (1, 128), 1)
    atoms = nuclei.shape[0]
    owner = lax.broadcasted_iota(jnp.int32, (atoms, 128), 0) == lax.div(
        lax.broadcasted_iota(jnp.int32, (atoms, 128), 1), 4
    )
    nuc = [
        jnp.sum(jnp.where(owner, nuclei[:, c : c + 1], 0.0), axis=0, keepdims=True)
        for c in range(3)
    ]
    kind = lax.rem(lane, 4)
    row_of = lax.broadcasted_iota(jnp.int32, (PAD, 3 * NE), 0)
    col_of = lax.broadcasted_iota(jnp.int32, (PAD, 3 * NE), 1)
    pick = [col_of == row_of * 3 + c for c in range(3)]
    live = lax.broadcasted_iota(jnp.int32, (PAD, 1), 0) < NE

    for s_from in range(S):
        for x_from in range(L):
            from_me = s_from * W + L * g + x_from == me

            @pl.when(jnp.logical_not(from_me))
            def _():
                walk_arrival(s_from, x_from).wait_recv()

    for s_to in range(S):
        for j_to in range(L):
            to_me = s_to * W + j_to * G + lax.div(w, L) == me

            @pl.when(jnp.logical_not(to_me))
            def _():
                walk_copy(s_to, j_to).wait_send()

    for i in range(N):
        for x in range(L):
            row = wbuf[i // L, x, i % L]
            pos = [
                jnp.sum(jnp.where(pick[c], row, 0.0), axis=1, keepdims=True) for c in range(3)
            ]
            off = [pos[c] - nuc[c] for c in range(3)]
            dist = jnp.sqrt(off[0] * off[0] + off[1] * off[1] + off[2] * off[2] + 1.0)
            f = jnp.where(
                kind == 0, off[0], jnp.where(kind == 1, off[1], jnp.where(kind == 2, off[2], dist))
            )
            p = i * L + x
            feats[p * PAD : (p + 1) * PAD, :] = f[:, :FEAT]

    head_of = lax.div(lax.broadcasted_iota(jnp.int32, (1, D), 1), head_size)
    head_mask = [jnp.where(head_of == h, 1.0, 0.0).astype(F32) for h in range(HEADS)]
    key_live = lax.broadcasted_iota(jnp.int32, (1, PAD), 1) < NE

    def stack_heads(x):
        return jnp.concatenate([x * head_mask[h] for h in range(HEADS)], axis=0)

    def merge_heads(x):
        return sum(x[h * PAD : (h + 1) * PAD] * head_mask[h] for h in range(HEADS))

    lrow[...] = jnp.zeros_like(lrow)

    def weights(n, parts):
        return [s_w[n, i] for i in range(parts)]

    def forward(b, carry):
        rows = pl.ds(pl.multiple_of(b * RB, RB), RB)
        h0 = product(split(feats[rows, :], 3), [s_embed[i] for i in range(3)], NN, 3)
        normed, scale = normalise(h0)
        x1[rows, :] = normed
        r1[rows, :] = scale
        xs = split(normed, 3)
        queries = product(xs, weights(0, 3), NN, 3)
        keys = product(xs, weights(1, 3), NN, 3)
        values = product(xs[:2], weights(2, 2), NN, 2)
        q[rows, :] = queries
        k[rows, :] = keys
        v[rows, :] = values
        ks = split(keys, 3)
        vs = split(values, 2)
        outs = []
        for i in range(WB):
            here = slice(i * PAD, (i + 1) * PAD)
            qs = split(stack_heads(queries[here]), 3)
            scores = product(qs, [piece[here] for piece in ks], NT, 3) / math.sqrt(head_size)
            scores = jnp.where(key_live, scores, -1e30)
            e = jnp.exp(scores - jnp.max(scores, axis=-1, keepdims=True))
            a = e / jnp.sum(e, axis=-1, keepdims=True)
            att[b * WB + i] = a
            outs.append(
                merge_heads(product(split(a, 2), [piece[here] for piece in vs], NN, 2))
            )
        mix = jnp.concatenate(outs, axis=0)
        mixed[rows, :] = mix
        h1 = h0 + product(split(mix, 2), weights(3, 2), NN, 2)
        normed2, scale2 = normalise(h1)
        x2[rows, :] = normed2
        r2[rows, :] = scale2
        t = jnp.tanh(product(split(normed2, 2), weights(4, 2), NN, 2) + vecs[0:1, :])
        act[rows, :] = t
        last = h1 + t
        h2[rows, :] = last
        out = last * vecs[1:2, :]
        for i in range(WB):
            here = slice(i * PAD, (i + 1) * PAD)
            value = jnp.sum(jnp.where(live, out[here], 0.0)) / NE
            lrow[...] += jnp.where(lane == b * WB + i, value, 0.0)
        return carry

    lax.fori_loop(0, blocks, forward, 0)

    def tab_copy(d):
        other = lax.rem(me + d, S * W)
        return pltpu.make_async_remote_copy(
            src_ref=lrow,
            dst_ref=tab.at[net, g],
            send_sem=tab_send.at[d],
            recv_sem=tab_recv.at[d],
            device_id=(lax.div(other, W), lax.rem(other, W)),
            device_id_type=MESH,
        )

    tab[net, g] = lrow[...]

    def start_tab(d, carry):
        tab_copy(d).start()
        return carry

    lax.fori_loop(1, S * W, start_tab, 0)

    def backward_top(b, carry):
        rows = pl.ds(pl.multiple_of(b * RB, RB), RB)
        gh = vecs[1:2, :] * (1.0 / NE)
        t = act[rows, :]
        dinner = gh * (1.0 - t * t)
        dx2 = product(split(dinner, 2), weights(4, 2), NT, 2)
        act[rows, :] = dinner
        dh1 = gh + normalise_back(dx2, x2[rows, :], r2[rows, :])
        g1[rows, :] = dh1
        dm[rows, :] = product(split(dh1, 2), weights(3, 2), NT, 2)
        return carry

    lax.fori_loop(0, blocks, backward_top, 0)

    def wait_tab(d, carry):
        other = lax.rem(me - d + S * W, S * W)
        wo = lax.rem(other, W)
        from_net = lax.div(other, W) * L + lax.div(wo, G)
        pltpu.make_async_remote_copy(
            src_ref=lrow,
            dst_ref=tab.at[from_net, lax.rem(wo, G)],
            send_sem=tab_send.at[d],
            recv_sem=tab_recv.at[d],
            device_id=(lax.div(other, W), wo),
            device_id_type=MESH,
        ).wait_recv()
        tab_copy(d).wait_send()
        return carry

    lax.fori_loop(1, S * W, wait_tab, 0)

    sub8 = lax.broadcasted_iota(jnp.int32, (N, 128), 0)
    lane8 = lax.broadcasted_iota(jnp.int32, (N, 128), 1)
    state8 = lax.div(lane8, L)
    home8 = jnp.where(state8 == sub8, 1.0, 0.0).astype(F32)
    ident = jnp.where(lane8 == sub8, 1.0, 0.0).astype(F32)

    def ratio_of(logs):
        logs = logs.reshape(N, 128)
        home = jnp.sum(logs * home8, axis=0, keepdims=True)
        return jnp.where(lane8 < held, jnp.exp(logs - home), 0.0)

    summed = ratio_of(tab[:, 0])
    for other in range(1, G):
        summed = summed + ratio_of(tab[:, other])
    coupled = jnp.zeros((N, 128), F32)
    table = jnp.zeros((N, 128), F32)
    for i in range(N):
        col = jnp.sum(jnp.where(state8 == i, summed, 0.0), axis=1, keepdims=True) / total_walkers
        coupled = jnp.where(sub8 == i, jnp.sum(col * home8, axis=0, keepdims=True), coupled)
        table = jnp.where(sub8 == i, jnp.sum(col * ident, axis=0, keepdims=True), table)
    margins[...] = table[:, :N]
    coupled = coupled * (1.0 - home8)
    ratio = ratio_of(tab[:, g])
    terms = coupled * ratio
    denominator = jnp.sum(terms, axis=0, keepdims=True)
    cot = (terms - home8 * denominator) / total_walkers
    cot = jnp.sum(jnp.where(sub8 == net, cot, 0.0), axis=0, keepdims=True)
    rows_of = lax.broadcasted_iota(jnp.int32, (held * PAD, 128), 0)
    first = lax.broadcasted_iota(jnp.int32, (held * PAD, 128), 1) * PAD
    inside = jnp.logical_and(rows_of >= first, rows_of < first + NE)
    ccol[...] = jnp.sum(jnp.where(inside, cot, 0.0), axis=1, keepdims=True)

    outs = (o_mlp, o_attn, o_value, o_key, o_query, o_extra)

    def rs_copy(m, d):
        to = lax.rem(g + d, G)
        if m < 5:
            src = part.at[m, pl.ds(pl.multiple_of(to * CH, CH), CH)]
            dst = rbuf.at[m, d - 1]
        else:
            src = part_extra.at[pl.ds(pl.multiple_of(to * EC, EC), EC)]
            dst = rbuf_extra.at[d - 1]
        return pltpu.make_async_remote_copy(
            src_ref=src,
            dst_ref=dst,
            send_sem=rs_send.at[m, d - 1],
            recv_sem=rs_recv.at[m, d - 1],
            device_id=(s, j * G + to),
            device_id_type=MESH,
        )

    def rs_start(m):
        for d in range(1, G):
            rs_copy(m, d).start()

    def piece(m, who):
        jj = lax.div(who, G)
        gg = lax.rem(who, G)
        if m < 5:
            return outs[m].at[jj, 0, pl.ds(pl.multiple_of(gg * CH, CH), CH)]
        return outs[m].at[jj, pl.ds(pl.multiple_of(gg * EC, EC), EC)]

    def rs_finish(m):
        for d in range(1, G):
            rs_copy(m, d).wait_recv()
        if m < 5:
            total = part[m, pl.ds(pl.multiple_of(g * CH, CH), CH)]
            for d in range(1, G):
                total = total + rbuf[m, d - 1]
            outs[m][j, 0, pl.ds(pl.multiple_of(g * CH, CH), CH)] = total
        else:
            total = part_extra[pl.ds(pl.multiple_of(g * EC, EC), EC)]
            for d in range(1, G):
                total = total + rbuf_extra[d - 1]
            outs[m][j, pl.ds(pl.multiple_of(g * EC, EC), EC)] = total

    odd = lax.rem(w, 2)
    place = (1 - odd) * lax.div(w, 2) + odd * (W - lax.div(w + 1, 2))

    def at_place(p):
        p = lax.rem(p + 2 * W, W)
        high = lax.div(p, W // 2)
        return (1 - high) * 2 * p + high * (2 * (W - p) - 1)

    def hops(m, way):
        return W // 2 if (m + way) % 2 == 0 else W - 1 - W // 2

    def ag_copy(m, way, t):
        step = 1 - 2 * way
        block = piece(m, at_place(place - step * t))
        return pltpu.make_async_remote_copy(
            src_ref=block,
            dst_ref=block,
            send_sem=ag_send.at[m, way, t],
            recv_sem=ag_recv.at[m, way, t],
            device_id=(s, at_place(place + step)),
            device_id_type=MESH,
        )

    def ag_arrival(m, way, t):
        step = 1 - 2 * way
        block = piece(m, at_place(place - step * (t + 1)))
        return pltpu.make_async_remote_copy(
            src_ref=block,
            dst_ref=block,
            send_sem=ag_send.at[m, way, t],
            recv_sem=ag_recv.at[m, way, t],
            device_id=(s, at_place(place - step)),
            device_id_type=MESH,
        )

    def ag_step(m, t):
        for way in range(2):
            if 0 < t <= hops(m, way):
                ag_arrival(m, way, t - 1).wait_recv()
            if t < hops(m, way):
                ag_copy(m, way, t).start()

    def ag_finish(m):
        for way in range(2):
            for t in range(hops(m, way)):
                ag_copy(m, way, t).wait_send()

    c = ccol[...]

    def outer(x, y):
        return product(split(x, 2), split(y * c, 2), TN, 2)

    part[0] = outer(x2[...], act[...])
    rs_start(0)
    part[1] = outer(mixed[...], g1[...])
    rs_start(1)

    def backward_attention(b, carry):
        rows = pl.ds(pl.multiple_of(b * RB, RB), RB)
        dq_list, dk_list, dv_list = [], [], []
        for i in range(WB):
            here = pl.ds(pl.multiple_of(b * RB + i * PAD, PAD), PAD)
            a = att[b * WB + i]
            dms = split(stack_heads(jnp.where(live, dm[here, :], 0.0)), 2)
            as_ = split(a, 2)
            vs = split(v[here, :], 2)
            ks = split(k[here, :], 2)
            qs = split(stack_heads(q[here, :]), 2)
            da = product(dms, vs, NT, 2)
            dv_list.append(product(as_, dms, TN, 2))
            ds = a * (da - jnp.sum(a * da, axis=-1, keepdims=True)) / math.sqrt(head_size)
            dss = split(ds, 2)
            dq_list.append(merge_heads(product(dss, ks, NN, 2)))
            dk_list.append(product(dss, qs, TN, 2))
        dq = jnp.concatenate(dq_list, axis=0)
        dk = jnp.concatenate(dk_list, axis=0)
        dv = jnp.concatenate(dv_list, axis=0)
        gq[rows, :] = dq
        gk[rows, :] = dk
        gv[rows, :] = dv
        dx1 = (
            product(split(dq, 2), weights(0, 2), NT, 2)
            + product(split(dk, 2), weights(1, 2), NT, 2)
            + product(split(dv, 2), weights(2, 2), NT, 2)
        )
        dm[rows, :] = g1[rows, :] + normalise_back(dx1, x1[rows, :], r1[rows, :])
        return carry

    lax.fori_loop(0, blocks, backward_attention, 0)

    part[2] = outer(x1[...], gv[...])
    rs_start(2)
    part[3] = outer(x1[...], gk[...])
    rs_start(3)
    part[4] = outer(x1[...], gq[...])
    rs_start(4)
    part_extra[...] = jnp.zeros_like(part_extra)
    part_extra[0:FEAT, :] = outer(feats[...], dm[...])
    part_extra[FEAT : FEAT + 1, :] = jnp.sum(act[...] * c, axis=0, keepdims=True)
    part_extra[FEAT + 1 : FEAT + 2, :] = jnp.sum(h2[...] * c, axis=0, keepdims=True) / NE
    rs_start(5)

    for m in range(6):
        rs_finish(m)
        ag_step(m, 0)
    for t in range(1, W // 2 + 1):
        for m in range(6):
            ag_step(m, t)
    for m in range(6):
        ag_finish(m)
        for d in range(1, G):
            rs_copy(m, d).wait_send()


def shards(walkers, nuclei, w_embed, w_query, w_key, w_value, w_attn_out, w_mlp, b_mlp, w_out):
    S = lax.axis_size("state")
    W = lax.axis_size("walker")
    L, per_device, coords = walkers.shape
    assert per_device == 1 and W % (2 * L) == 0
    G = W // L
    N = S * L
    NE = coords // 3
    PAD = -(-NE // 16) * 16
    FEAT, D = w_embed.shape[1:]
    CH = D // G
    rows_extra = max(-(-(FEAT + 2) // (8 * G)) * 8 * G, 8 * G)
    EC = rows_extra // G
    held = N * L
    R = held * PAD
    cfg = (S, W, L, G, N, NE, PAD, D, FEAT, CH, EC)
    vmem = pl.BlockSpec(memory_space=pltpu.VMEM)
    hbm = pl.BlockSpec(memory_space=pl.ANY)
    full = lambda: pltpu.VMEM((R, D), F32)
    column = lambda: pltpu.VMEM((R, 1), F32)
    weight = jax.ShapeDtypeStruct((L, 1, D, D), F32)
    dma = pltpu.SemaphoreType.DMA
    outs = pl.pallas_call(
        functools.partial(kernel, cfg),
        out_shape=(
            jax.ShapeDtypeStruct((N, N), F32),
            weight, weight, weight, weight, weight,
            jax.ShapeDtypeStruct((L, rows_extra, D), F32),
        ),
        in_specs=[vmem, vmem, hbm, hbm, hbm, hbm, hbm, hbm, vmem, vmem],
        out_specs=(vmem,) * 7,
        scratch_shapes=[
            pltpu.VMEM((S, L, L, 1, coords), F32),
            pltpu.VMEM((FEAT, D), F32),
            pltpu.VMEM((5, D, D), F32),
            pltpu.VMEM((8, D), F32),
            pltpu.VMEM((3, FEAT, D), BF16),
            pltpu.VMEM((5, 3, D, D), BF16),
            pltpu.VMEM((R, FEAT), F32),
            full(), column(), full(), full(), full(),
            pltpu.VMEM((held, HEADS * PAD, PAD), F32),
            full(), full(), column(), full(), full(),
            full(), full(), full(), full(), full(),
            pltpu.VMEM((1, 128), F32),
            pltpu.VMEM((N, G, 1, 128), F32),
            pltpu.VMEM((5, D, D), F32),
            pltpu.VMEM((rows_extra, D), F32),
            pltpu.VMEM((5, G - 1, CH, D), F32),
            pltpu.VMEM((G - 1, EC, D), F32),
            column(),
            dma((6,)),
            dma((S, L)), dma((S, L)),
            dma((S * W,)), dma((S * W,)),
            dma((6, G - 1)), dma((6, G - 1)),
            dma((6, 2, W // 2)), dma((6, 2, W // 2)),
        ],
        compiler_params=pltpu.CompilerParams(
            collective_id=0, has_side_effects=True, vmem_limit_bytes=56 * 1024 * 1024
        ),
    )(walkers, nuclei, w_embed, w_query, w_key, w_value, w_attn_out, w_mlp, b_mlp, w_out)
    margins, g_query, g_key, g_value, g_attn, g_mlp, extra = outs
    return (
        margins,
        extra[:, :FEAT],
        g_query, g_key, g_value, g_attn, g_mlp,
        extra[:, FEAT : FEAT + 1],
        extra[:, FEAT + 1],
    )


def solution(mesh):
    return jax.shard_map(
        shards,
        mesh=mesh,
        in_specs=(
            P("state", "walker", None),
            P(),
            P("state", None, None),
            P("state", None, None, None),
            P("state", None, None, None),
            P("state", None, None, None),
            P("state", None, None, None),
            P("state", None, None, None),
            P("state", None, None),
            P("state", None),
        ),
        out_specs=(
            P(),
            P("state", None, None),
            P("state", None, None, None),
            P("state", None, None, None),
            P("state", None, None, None),
            P("state", None, None, None),
            P("state", None, None, None),
            P("state", None, None),
            P("state", None),
        ),
        check_vma=False,
    )
```

```python
import functools
import math

import jax
import jax.numpy as jnp
from jax import lax
from jax.experimental import pallas as pl
from jax.experimental.pallas import tpu as pltpu
from jax.sharding import PartitionSpec as P

HEADS = 4
EPS = 1e-05
F32 = jnp.float32
BF16 = jnp.bfloat16
MESH = pl.DeviceIdType.MESH
WALKERS_PER_BLOCK = 4

NN = (((1,), (0,)), ((), ()))
NT = (((1,), (1,)), ((), ()))
TN = (((0,), (0,)), ((), ()))


def split(x, parts):
    out = []
    for part in range(parts):
        piece = x.astype(BF16)
        out.append(piece)
        if part + 1 < parts:
            x = x - piece.astype(F32)
    return out


def product(a, b, dims, parts):
    total = None
    for order in range(parts - 1, -1, -1):
        for i in range(order + 1):
            term = lax.dot_general(a[i], b[order - i], dims, preferred_element_type=F32)
            total = term if total is None else total + term
    return total


def product_packed(a, b):
    parts, width = len(a), b[0].shape[0]
    stack = jnp.concatenate(b, axis=0)
    sums = [None] * parts
    for i in range(parts - 1, -1, -1):
        wide = lax.dot_general(
            a[i], stack[: (parts - i) * width], NT, preferred_element_type=F32
        )
        for n in range(parts - i):
            term = wide[:, n * width : (n + 1) * width]
            sums[i + n] = term if sums[i + n] is None else sums[i + n] + term
    total = sums[-1]
    for term in sums[-2::-1]:
        total = total + term
    return total


def normalise(hidden):
    centre = hidden - jnp.mean(hidden, axis=-1, keepdims=True)
    spread = jnp.mean(centre * centre, axis=-1, keepdims=True)
    scale = 1.0 / jnp.sqrt(spread + EPS)
    return centre * scale, scale


def normalise_back(grad, normed, scale):
    mean = jnp.mean(grad, axis=-1, keepdims=True)
    along = jnp.mean(grad * normed, axis=-1, keepdims=True)
    return scale * (grad - mean - normed * along)


def kernel(
    cfg,
    walkers, nuclei_in, w_embed, w_query, w_key, w_value, w_attn, w_mlp, b_mlp_in, w_out_in,
    margins, f_mlp, f_attn, f_value, f_key, f_query, f_extra,
    o_weights, o_extra, nuclei, b_mlp, w_out, wbuf, raw_embed, raw, vecs, s_embed, s_w, feats, x1, r1, q, k, v, att, mixed, x2, r2, act, h2,
    g1, gk, gq, gv, dm, lrow, tab, part, part_extra, rbuf, rbuf_extra, ccol,
    load_sem, flush_sem, walk_send, walk_recv, tab_send, tab_recv, rs_send, rs_recv, ag_send, ag_recv,
):
    S, W, L, G, N, NE, PAD, D, FEAT, CH, EC = cfg
    held = N * L
    head_size = D // HEADS
    WB = WALKERS_PER_BLOCK
    RB = WB * PAD
    blocks = held // WB
    total_walkers = W
    s = lax.axis_index("state")
    w = lax.axis_index("walker")
    j = lax.div(w, G)
    g = lax.rem(w, G)
    net = s * L + j
    me = s * W + w

    loads = [pltpu.make_async_copy(w_embed.at[j], raw_embed, load_sem.at[0])]
    for n, ref in enumerate((w_query, w_key, w_value, w_attn, w_mlp)):
        loads.append(pltpu.make_async_copy(ref.at[j, 0], raw.at[n], load_sem.at[1 + n]))
    for n, (src, dst) in enumerate(((nuclei_in, nuclei), (b_mlp_in, b_mlp), (w_out_in, w_out))):
        loads.append(pltpu.make_async_copy(src, dst, load_sem.at[6 + n]))
    for copy in loads:
        copy.start()

    barrier = pltpu.get_barrier_semaphore()

    def greet(d, carry):
        other = lax.rem(me + d, S * W)
        pl.semaphore_signal(
            barrier, inc=1, device_id=(lax.div(other, W), lax.rem(other, W)), device_id_type=MESH
        )
        return carry

    lax.fori_loop(1, S * W, greet, 0)

    for copy in loads:
        copy.wait()
    for i, piece in enumerate(split(raw_embed[...], 3)):
        s_embed[i] = piece
    for n in range(5):
        for i, piece in enumerate(split(raw[n], 3 if n < 2 else 2)):
            s_w[n, i] = piece
    vecs[0:1, :] = b_mlp[j]
    vecs[1:2, :] = w_out[pl.ds(j, 1), :]

    pl.semaphore_wait(barrier, S * W - 1)

    def walk_copy(s_to, j_to):
        return pltpu.make_async_remote_copy(
            src_ref=walkers,
            dst_ref=wbuf.at[s, lax.rem(w, L)],
            send_sem=walk_send.at[s_to, j_to],
            recv_sem=walk_recv.at[s, lax.rem(w, L)],
            device_id=(s_to, j_to * G + lax.div(w, L)),
            device_id_type=MESH,
        )

    def walk_arrival(s_from, x_from):
        return pltpu.make_async_remote_copy(
            src_ref=walkers,
            dst_ref=wbuf.at[s_from, x_from],
            send_sem=walk_send.at[0, 0],
            recv_sem=walk_recv.at[s_from, x_from],
            device_id=(s_from, L * g + x_from),
            device_id_type=MESH,
        )

    for s_to in range(S):
        for j_to in range(L):
            to_me = s_to * W + j_to * G + lax.div(w, L) == me

            @pl.when(jnp.logical_not(to_me))
            def _():
                walk_copy(s_to, j_to).start()

            @pl.when(to_me)
            def _():
                own = pltpu.make_async_copy(walkers, wbuf.at[s, lax.rem(w, L)], load_sem.at[9])
                own.start()
                own.wait()

    lane = lax.broadcasted_iota(jnp.int32, (1, 128), 1)
    atom = lax.div(lane, 4)
    nuc = []
    for c in range(3):
        along = jnp.zeros((1, 128), F32)
        for a in range(nuclei.shape[1]):
            along = jnp.where(atom == a, nuclei[c : c + 1, a : a + 1], along)
        nuc.append(along)
    kind = lax.rem(lane, 4)
    row_of = lax.broadcasted_iota(jnp.int32, (PAD, 3 * NE), 0)
    col_of = lax.broadcasted_iota(jnp.int32, (PAD, 3 * NE), 1)
    pick = [col_of == row_of * 3 + c for c in range(3)]
    live = lax.broadcasted_iota(jnp.int32, (PAD, 1), 0) < NE

    for s_from in range(S):
        for x_from in range(L):
            from_me = s_from * W + L * g + x_from == me

            @pl.when(jnp.logical_not(from_me))
            def _():
                walk_arrival(s_from, x_from).wait_recv()

    for s_to in range(S):
        for j_to in range(L):
            to_me = s_to * W + j_to * G + lax.div(w, L) == me

            @pl.when(jnp.logical_not(to_me))
            def _():
                walk_copy(s_to, j_to).wait_send()

    for i in range(N):
        for x in range(L):
            row = wbuf[i // L, x, i % L]
            pos = [
                jnp.sum(jnp.where(pick[c], row, 0.0), axis=1, keepdims=True) for c in range(3)
            ]
            off = [pos[c] - nuc[c] for c in range(3)]
            dist = jnp.sqrt(off[0] * off[0] + off[1] * off[1] + off[2] * off[2] + 1.0)
            f = jnp.where(
                kind == 0, off[0], jnp.where(kind == 1, off[1], jnp.where(kind == 2, off[2], dist))
            )
            p = i * L + x
            feats[p * PAD : (p + 1) * PAD, :] = f[:, :FEAT]

    head_of = lax.div(lax.broadcasted_iota(jnp.int32, (1, D), 1), head_size)
    head_mask = [jnp.where(head_of == h, 1.0, 0.0).astype(F32) for h in range(HEADS)]
    head_mask_bf16 = [mask.astype(BF16) for mask in head_mask]
    key_live = lax.broadcasted_iota(jnp.int32, (1, PAD), 1) < NE

    def stack_heads(x):
        return jnp.concatenate([x * head_mask_bf16[h] for h in range(HEADS)], axis=0)

    def merge_heads(x):
        return sum(x[h * PAD : (h + 1) * PAD] * head_mask[h] for h in range(HEADS))

    lrow[...] = jnp.zeros_like(lrow)

    def weights(n, parts):
        return [s_w[n, i] for i in range(parts)]

    def forward(b, carry):
        rows = pl.ds(pl.multiple_of(b * RB, RB), RB)
        h0 = product(split(feats[rows, :], 3), [s_embed[i] for i in range(3)], NN, 3)
        normed, scale = normalise(h0)
        x1[rows, :] = normed
        r1[rows, :] = scale
        xs = split(normed, 3)
        queries = product(xs, weights(0, 3), NN, 3)
        keys = product(xs, weights(1, 3), NN, 3)
        values = product(xs[:2], weights(2, 2), NN, 2)
        q[rows, :] = queries
        k[rows, :] = keys
        v[rows, :] = values
        queries_split = split(queries, 3)
        ks = split(keys, 3)
        vs = split(values, 2)
        outs = []
        for i in range(WB):
            here = slice(i * PAD, (i + 1) * PAD)
            qs = [stack_heads(piece[here]) for piece in queries_split]
            scores = product_packed(qs, [piece[here] for piece in ks]) / math.sqrt(head_size)
            scores = jnp.where(key_live, scores, -1e30)
            e = jnp.exp(scores - jnp.max(scores, axis=-1, keepdims=True))
            a = e / jnp.sum(e, axis=-1, keepdims=True)
            att[b * WB + i] = a
            outs.append(
                merge_heads(product(split(a, 2), [piece[here] for piece in vs], NN, 2))
            )
        mix = jnp.concatenate(outs, axis=0)
        mixed[rows, :] = mix
        h1 = h0 + product(split(mix, 2), weights(3, 2), NN, 2)
        normed2, scale2 = normalise(h1)
        x2[rows, :] = normed2
        r2[rows, :] = scale2
        t = jnp.tanh(product(split(normed2, 2), weights(4, 2), NN, 2) + vecs[0:1, :])
        act[rows, :] = t
        last = h1 + t
        h2[rows, :] = last
        out = last * vecs[1:2, :]
        for i in range(WB):
            here = slice(i * PAD, (i + 1) * PAD)
            value = jnp.sum(jnp.where(live, out[here], 0.0)) / NE
            lrow[...] += jnp.where(lane == b * WB + i, value, 0.0)
        return carry

    lax.fori_loop(0, blocks, forward, 0)

    def tab_copy(d):
        other = lax.rem(me + d, S * W)
        return pltpu.make_async_remote_copy(
            src_ref=lrow,
            dst_ref=tab.at[net, g],
            send_sem=tab_send.at[d],
            recv_sem=tab_recv.at[d],
            device_id=(lax.div(other, W), lax.rem(other, W)),
            device_id_type=MESH,
        )

    tab[net, g] = lrow[...]

    def start_tab(d, carry):
        tab_copy(d).start()
        return carry

    lax.fori_loop(1, S * W, start_tab, 0)

    def backward_top(b, carry):
        rows = pl.ds(pl.multiple_of(b * RB, RB), RB)
        gh = vecs[1:2, :] * (1.0 / NE)
        t = act[rows, :]
        dinner = gh * (1.0 - t * t)
        dx2 = product(split(dinner, 2), weights(4, 2), NT, 2)
        act[rows, :] = dinner
        dh1 = gh + normalise_back(dx2, x2[rows, :], r2[rows, :])
        g1[rows, :] = dh1
        dm[rows, :] = product(split(dh1, 2), weights(3, 2), NT, 2)
        return carry

    lax.fori_loop(0, blocks, backward_top, 0)

    def wait_tab(d, carry):
        other = lax.rem(me - d + S * W, S * W)
        wo = lax.rem(other, W)
        from_net = lax.div(other, W) * L + lax.div(wo, G)
        pltpu.make_async_remote_copy(
            src_ref=lrow,
            dst_ref=tab.at[from_net, lax.rem(wo, G)],
            send_sem=tab_send.at[d],
            recv_sem=tab_recv.at[d],
            device_id=(lax.div(other, W), wo),
            device_id_type=MESH,
        ).wait_recv()
        tab_copy(d).wait_send()
        return carry

    lax.fori_loop(1, S * W, wait_tab, 0)

    sub8 = lax.broadcasted_iota(jnp.int32, (N, 128), 0)
    lane8 = lax.broadcasted_iota(jnp.int32, (N, 128), 1)
    state8 = lax.div(lane8, L)
    home8 = jnp.where(state8 == sub8, 1.0, 0.0).astype(F32)
    ident = jnp.where(lane8 == sub8, 1.0, 0.0).astype(F32)

    def ratio_of(logs):
        logs = logs.reshape(N, 128)
        home = jnp.sum(logs * home8, axis=0, keepdims=True)
        return jnp.where(lane8 < held, jnp.exp(logs - home), 0.0)

    summed = ratio_of(tab[:, 0])
    for other in range(1, G):
        summed = summed + ratio_of(tab[:, other])
    coupled = jnp.zeros((N, 128), F32)
    table = jnp.zeros((N, 128), F32)
    for i in range(N):
        col = jnp.sum(jnp.where(state8 == i, summed, 0.0), axis=1, keepdims=True) / total_walkers
        coupled = jnp.where(sub8 == i, jnp.sum(col * home8, axis=0, keepdims=True), coupled)
        table = jnp.where(sub8 == i, jnp.sum(col * ident, axis=0, keepdims=True), table)
    margins[...] = table[:, :N]
    coupled = coupled * (1.0 - home8)
    ratio = ratio_of(tab[:, g])
    terms = coupled * ratio
    denominator = jnp.sum(terms, axis=0, keepdims=True)
    cot = (terms - home8 * denominator) / total_walkers
    cot = jnp.sum(jnp.where(sub8 == net, cot, 0.0), axis=0, keepdims=True)
    rows_of = lax.broadcasted_iota(jnp.int32, (held * PAD, 128), 0)
    first = lax.broadcasted_iota(jnp.int32, (held * PAD, 128), 1) * PAD
    inside = jnp.logical_and(rows_of >= first, rows_of < first + NE)
    ccol[...] = jnp.sum(jnp.where(inside, cot, 0.0), axis=1, keepdims=True)

    outs = [o_weights.at[m] for m in range(5)] + [o_extra]
    results = (f_mlp, f_attn, f_value, f_key, f_query, f_extra)

    def rs_copy(m, d):
        to = lax.rem(g + d, G)
        if m < 5:
            src = part.at[m, pl.ds(pl.multiple_of(to * CH, CH), CH)]
            dst = rbuf.at[m, d - 1]
        else:
            src = part_extra.at[pl.ds(pl.multiple_of(to * EC, EC), EC)]
            dst = rbuf_extra.at[d - 1]
        return pltpu.make_async_remote_copy(
            src_ref=src,
            dst_ref=dst,
            send_sem=rs_send.at[m, d - 1],
            recv_sem=rs_recv.at[m, d - 1],
            device_id=(s, j * G + to),
            device_id_type=MESH,
        )

    def rs_start(m):
        for d in range(1, G):
            rs_copy(m, d).start()

    def piece(m, who):
        jj = lax.div(who, G)
        gg = lax.rem(who, G)
        if m < 5:
            return outs[m].at[jj, 0, pl.ds(pl.multiple_of(gg * CH, CH), CH)]
        return outs[m].at[jj, pl.ds(pl.multiple_of(gg * EC, EC), EC)]

    def rs_finish(m):
        for d in range(1, G):
            rs_copy(m, d).wait_recv()
        if m < 5:
            total = part[m, pl.ds(pl.multiple_of(g * CH, CH), CH)]
            for d in range(1, G):
                total = total + rbuf[m, d - 1]
            outs[m][j, 0, pl.ds(pl.multiple_of(g * CH, CH), CH)] = total
        else:
            total = part_extra[pl.ds(pl.multiple_of(g * EC, EC), EC)]
            for d in range(1, G):
                total = total + rbuf_extra[d - 1]
            outs[m][j, pl.ds(pl.multiple_of(g * EC, EC), EC)] = total

    odd = lax.rem(w, 2)
    place = (1 - odd) * lax.div(w, 2) + odd * (W - lax.div(w + 1, 2))

    def at_place(p):
        p = lax.rem(p + 2 * W, W)
        high = lax.div(p, W // 2)
        return (1 - high) * 2 * p + high * (2 * (W - p) - 1)

    def hops(m, way):
        return W // 2 if (m + way) % 2 == 0 else W - 1 - W // 2

    def ag_copy(m, way, t):
        step = 1 - 2 * way
        block = piece(m, at_place(place - step * t))
        return pltpu.make_async_remote_copy(
            src_ref=block,
            dst_ref=block,
            send_sem=ag_send.at[m, way, t],
            recv_sem=ag_recv.at[m, way, t],
            device_id=(s, at_place(place + step)),
            device_id_type=MESH,
        )

    def ag_arrival(m, way, t):
        step = 1 - 2 * way
        block = piece(m, at_place(place - step * (t + 1)))
        return pltpu.make_async_remote_copy(
            src_ref=block,
            dst_ref=block,
            send_sem=ag_send.at[m, way, t],
            recv_sem=ag_recv.at[m, way, t],
            device_id=(s, at_place(place - step)),
            device_id_type=MESH,
        )

    def ag_step(m, t):
        for way in range(2):
            if 0 < t <= hops(m, way):
                ag_arrival(m, way, t - 1).wait_recv()
            if t < hops(m, way):
                ag_copy(m, way, t).start()
        if t == last:
            flush(m).start()

    last = W // 2

    def flush(m):
        return pltpu.make_async_copy(outs[m], results[m], flush_sem.at[m])

    def ag_finish(m):
        for way in range(2):
            for t in range(hops(m, way)):
                ag_copy(m, way, t).wait_send()
        flush(m).wait()

    todo = [[("sum", 0)] + [("hop", t) for t in range(1, last + 1)] for m in range(6)]

    def advance(*arrays):
        for m in arrays:
            if todo[m]:
                what, t = todo[m].pop(0)
                if what == "sum":
                    rs_finish(m)
                ag_step(m, t)

    c = ccol[...]

    def outer(x, y):
        return product(split(x, 2), split(y * c, 2), TN, 2)

    part[0] = outer(x2[...], act[...])
    rs_start(0)
    part[1] = outer(mixed[...], g1[...])
    rs_start(1)

    def stacked_gradient(here):
        return [stack_heads(p) for p in split(jnp.where(live, dm[here, :], 0.0), 2)]

    def backward_values(b, carry):
        for i in range(WB):
            here = pl.ds(pl.multiple_of(b * RB + i * PAD, PAD), PAD)
            gv[here, :] = product(split(att[b * WB + i], 2), stacked_gradient(here), TN, 2)
        return carry

    lax.fori_loop(0, blocks, backward_values, 0)
    part[2] = outer(x1[...], gv[...])
    rs_start(2)
    advance(0)
    advance(1)

    def backward_scores(b, carry):
        for i in range(WB):
            here = pl.ds(pl.multiple_of(b * RB + i * PAD, PAD), PAD)
            a = att[b * WB + i]
            ks = split(k[here, :], 2)
            qs = [stack_heads(p) for p in split(q[here, :], 2)]
            da = product_packed(stacked_gradient(here), split(v[here, :], 2))
            ds = a * (da - jnp.sum(a * da, axis=-1, keepdims=True)) / math.sqrt(head_size)
            dss = split(ds, 2)
            gq[here, :] = merge_heads(product(dss, ks, NN, 2))
            gk[here, :] = product(dss, qs, TN, 2)

        for bb in range(blocks):
            arrays = ((0, 2), (0, 1), (0, 1, 2), (0, 1, 2))[bb % 4] if bb < 4 else ()

            @pl.when(b == bb)
            def _():
                advance(*arrays)

        return carry

    lax.fori_loop(0, blocks, backward_scores, 0)

    part[3] = outer(x1[...], gk[...])
    rs_start(3)
    part[4] = outer(x1[...], gq[...])
    rs_start(4)
    advance(1, 2)

    def backward_embed(b, carry):
        rows = pl.ds(pl.multiple_of(b * RB, RB), RB)
        dx1 = (
            product(split(gq[rows, :], 2), weights(0, 2), NT, 2)
            + product(split(gk[rows, :], 2), weights(1, 2), NT, 2)
            + product(split(gv[rows, :], 2), weights(2, 2), NT, 2)
        )
        dm[rows, :] = g1[rows, :] + normalise_back(dx1, x1[rows, :], r1[rows, :])
        return carry

    lax.fori_loop(0, blocks, backward_embed, 0)
    advance(3, 4, 2)
    part_extra[...] = jnp.zeros_like(part_extra)
    part_extra[0:FEAT, :] = outer(feats[...], dm[...])
    part_extra[FEAT : FEAT + 1, :] = jnp.sum(act[...] * c, axis=0, keepdims=True)
    part_extra[FEAT + 1 : FEAT + 2, :] = jnp.sum(h2[...] * c, axis=0, keepdims=True) / NE
    rs_start(5)
    advance(3, 4)
    while any(todo):
        advance(*range(6))
    for m in range(6):
        ag_finish(m)
        for d in range(1, G):
            rs_copy(m, d).wait_send()


def finish_kernel(
    m_in, mlp, attn, value, key, query, extra,
    margins, o_embed, o_query, o_key, o_value, o_attn, o_mlp, o_bias, o_out, sem,
):
    feat = o_embed.shape[1]
    margins[...] = m_in[...]
    copies = []
    for src, dst in ((query, o_query), (key, o_key), (value, o_value), (attn, o_attn), (mlp, o_mlp)):
        for n in range(dst.shape[0]):
            copies.append(pltpu.make_async_copy(src.at[n], dst.at[n], sem.at[len(copies)]))
    for copy in copies:
        copy.start()
    for n in range(o_embed.shape[0]):
        o_embed[n] = extra[n, :feat]
        o_bias[n] = extra[n, feat : feat + 1]
        o_out[n : n + 1, :] = extra[n, feat + 1 : feat + 2]
    for copy in copies:
        copy.wait()


def shards(walkers, nuclei, w_embed, w_query, w_key, w_value, w_attn_out, w_mlp, b_mlp, w_out):
    S = lax.axis_size("state")
    W = lax.axis_size("walker")
    L, per_device, coords = walkers.shape
    assert per_device == 1 and W % (2 * L) == 0
    G = W // L
    N = S * L
    NE = coords // 3
    PAD = -(-NE // 16) * 16
    FEAT, D = w_embed.shape[1:]
    CH = D // G
    rows_extra = max(-(-(FEAT + 2) // (8 * G)) * 8 * G, 8 * G)
    EC = rows_extra // G
    held = N * L
    R = held * PAD
    cfg = (S, W, L, G, N, NE, PAD, D, FEAT, CH, EC)
    vmem = pl.BlockSpec(memory_space=pltpu.VMEM)
    hbm = pl.BlockSpec(memory_space=pl.ANY)
    full = lambda: pltpu.VMEM((R, D), F32)
    column = lambda: pltpu.VMEM((R, 1), F32)
    weight = jax.ShapeDtypeStruct((L, 1, D, D), F32)
    dma = pltpu.SemaphoreType.DMA
    outs = pl.pallas_call(
        functools.partial(kernel, cfg),
        out_shape=(
            jax.ShapeDtypeStruct((N, N), F32),
            weight, weight, weight, weight, weight,
            jax.ShapeDtypeStruct((L, rows_extra, D), F32),
        ),
        in_specs=[hbm] * 10,
        out_specs=(vmem,) + (hbm,) * 6,
        scratch_shapes=[
            pltpu.VMEM((5, L, 1, D, D), F32),
            pltpu.VMEM((L, rows_extra, D), F32),
            pltpu.VMEM(nuclei.shape[::-1], F32),
            pltpu.VMEM(b_mlp.shape, F32),
            pltpu.VMEM(w_out.shape, F32),
            pltpu.VMEM((S, L, L, 1, coords), F32),
            pltpu.VMEM((FEAT, D), F32),
            pltpu.VMEM((5, D, D), F32),
            pltpu.VMEM((8, D), F32),
            pltpu.VMEM((3, FEAT, D), BF16),
            pltpu.VMEM((5, 3, D, D), BF16),
            pltpu.VMEM((R, FEAT), F32),
            full(), column(), full(), full(), full(),
            pltpu.VMEM((held, HEADS * PAD, PAD), F32),
            full(), full(), column(), full(), full(),
            full(), full(), full(), full(), full(),
            pltpu.VMEM((1, 128), F32),
            pltpu.VMEM((N, G, 1, 128), F32),
            pltpu.VMEM((5, D, D), F32),
            pltpu.VMEM((rows_extra, D), F32),
            pltpu.VMEM((5, G - 1, CH, D), F32),
            pltpu.VMEM((G - 1, EC, D), F32),
            column(),
            dma((10,)), dma((6,)),
            dma((S, L)), dma((S, L)),
            dma((S * W,)), dma((S * W,)),
            dma((6, G - 1)), dma((6, G - 1)),
            dma((6, 2, W // 2)), dma((6, 2, W // 2)),
        ],
        compiler_params=pltpu.CompilerParams(
            collective_id=0, has_side_effects=True, vmem_limit_bytes=56 * 1024 * 1024
        ),
    )(walkers, nuclei.T, w_embed, w_query, w_key, w_value, w_attn_out, w_mlp, b_mlp, w_out)
    like = lambda x: jax.ShapeDtypeStruct(x.shape, F32)
    return pl.pallas_call(
        finish_kernel,
        out_shape=(
            jax.ShapeDtypeStruct((N, N), F32),
            like(w_embed), weight, weight, weight, weight, weight, like(b_mlp), like(w_out),
        ),
        in_specs=[vmem] + [hbm] * 5 + [vmem],
        out_specs=(vmem, vmem) + (hbm,) * 5 + (vmem, vmem),
        scratch_shapes=[dma((5 * L,))],
        compiler_params=pltpu.CompilerParams(vmem_limit_bytes=56 * 1024 * 1024),
    )(*outs)


def solution(mesh):
    return jax.shard_map(
        shards,
        mesh=mesh,
        in_specs=(
            P("state", "walker", None),
            P(),
            P("state", None, None),
            P("state", None, None, None),
            P("state", None, None, None),
            P("state", None, None, None),
            P("state", None, None, None),
            P("state", None, None, None),
            P("state", None, None),
            P("state", None),
        ),
        out_specs=(
            P(),
            P("state", None, None),
            P("state", None, None, None),
            P("state", None, None, None),
            P("state", None, None, None),
            P("state", None, None, None),
            P("state", None, None, None),
            P("state", None, None),
            P("state", None),
        ),
        check_vma=False,
    )
```

```python
import functools
import math

import jax
import jax.numpy as jnp
from jax import lax
from jax.experimental import pallas as pl
from jax.experimental.pallas import tpu as pltpu
from jax.sharding import PartitionSpec as P

HEADS = 4
EPS = 1e-05
F32 = jnp.float32
BF16 = jnp.bfloat16
MESH = pl.DeviceIdType.MESH
WALKERS_PER_BLOCK = 8

NN = (((1,), (0,)), ((), ()))
NT = (((1,), (1,)), ((), ()))
TN = (((0,), (0,)), ((), ()))


def split(x, parts):
    out = []
    for part in range(parts):
        piece = x.astype(BF16)
        out.append(piece)
        if part + 1 < parts:
            x = x - piece.astype(F32)
    return out


def terms(parts):
    return [(i, order - i) for order in range(parts - 1, -1, -1) for i in range(order + 1)]


def left(x, parts):
    pieces = split(x, parts)
    return jnp.concatenate([pieces[i] for i, _ in terms(parts)], axis=1)


def right(x, parts):
    pieces = split(x, parts)
    return jnp.concatenate([pieces[i] for _, i in terms(parts)], axis=0)


def matmul(a, b, dims=NN):
    return lax.dot_general(a, b, dims, preferred_element_type=F32)


def product(a, b, dims):
    parts, rows = len(a), a[0].shape[0]
    sums = [None] * parts
    for n in range(parts - 1, -1, -1):
        tall = matmul(jnp.concatenate(a[: parts - n], axis=0), b[n], dims)
        for i in range(parts - n):
            term = tall[i * rows : (i + 1) * rows]
            sums[i + n] = term if sums[i + n] is None else sums[i + n] + term
    total = sums[-1]
    for term in sums[-2::-1]:
        total = total + term
    return total


def normalise(hidden):
    centre = hidden - jnp.mean(hidden, axis=-1, keepdims=True)
    spread = jnp.mean(centre * centre, axis=-1, keepdims=True)
    scale = 1.0 / jnp.sqrt(spread + EPS)
    return centre * scale, scale


def normalise_back(grad, normed, scale):
    mean = jnp.mean(grad, axis=-1, keepdims=True)
    along = jnp.mean(grad * normed, axis=-1, keepdims=True)
    return scale * (grad - mean - normed * along)


def kernel(
    cfg,
    walkers, nuclei_in, w_embed, w_query, w_key, w_value, w_attn, w_mlp, b_mlp_in, w_out_in,
    margins, f_mlp, f_attn, f_value, f_key, f_query, f_extra,
    o_weights, o_extra, nuclei, b_mlp, w_out, wbuf, raw_embed, raw, vecs, s_embed, s_qk, s_w, s_qkvt, s_t, spots, feats, x1, r1, q, k, v, att, mixed, x2, r2, act, h2,
    g1, gk, gq, gv, dm, lrow, tab, part, part_extra, rbuf, rbuf_extra, ccol,
    load_sem, flush_sem, walk_send, walk_recv, tab_send, tab_recv, rs_send, rs_recv, ag_send, ag_recv,
):
    S, W, L, G, N, NE, PAD, D, FEAT, CH, EC = cfg
    held = N * L
    head_size = D // HEADS
    WB = WALKERS_PER_BLOCK
    RB = WB * PAD
    blocks = held // WB
    total_walkers = W
    s = lax.axis_index("state")
    w = lax.axis_index("walker")
    j = lax.div(w, G)
    g = lax.rem(w, G)
    net = s * L + j
    me = s * W + w

    loads = [pltpu.make_async_copy(w_embed.at[j], raw_embed.at[pl.ds(0, FEAT)], load_sem.at[0])]
    for n, ref in enumerate((w_query, w_key, w_value, w_attn, w_mlp)):
        loads.append(pltpu.make_async_copy(ref.at[j, 0], raw.at[n], load_sem.at[1 + n]))
    for n, (src, dst) in enumerate(((nuclei_in, nuclei), (b_mlp_in, b_mlp), (w_out_in, w_out))):
        loads.append(pltpu.make_async_copy(src, dst, load_sem.at[6 + n]))
    for copy in loads:
        copy.start()

    barrier = pltpu.get_barrier_semaphore()

    def greet(d, carry):
        other = lax.rem(me + d, S * W)
        pl.semaphore_signal(
            barrier, inc=1, device_id=(lax.div(other, W), lax.rem(other, W)), device_id_type=MESH
        )
        return carry

    lax.fori_loop(1, S * W, greet, 0)

    raw_embed[FEAT:, :] = jnp.zeros((128 - FEAT, D), F32)
    for copy in loads:
        copy.wait()
    s_embed[...] = right(raw_embed[...], 3)
    s_qk[...] = jnp.concatenate([right(raw[0], 3), right(raw[1], 3)], axis=1)
    for n in range(3):
        s_w[n] = right(raw[2 + n], 2)
        s_qkvt[n] = right(raw[n].T, 2)
    for n in range(2):
        s_t[n] = right(raw[3 + n].T, 2)
    vecs[0:1, :] = b_mlp[j]
    vecs[1:2, :] = w_out[pl.ds(j, 1), :]

    pl.semaphore_wait(barrier, S * W - 1)

    def walk_copy(s_to, j_to):
        return pltpu.make_async_remote_copy(
            src_ref=walkers,
            dst_ref=wbuf.at[s, lax.rem(w, L)],
            send_sem=walk_send.at[s_to, j_to],
            recv_sem=walk_recv.at[s, lax.rem(w, L)],
            device_id=(s_to, j_to * G + lax.div(w, L)),
            device_id_type=MESH,
        )

    def walk_arrival(s_from, x_from):
        return pltpu.make_async_remote_copy(
            src_ref=walkers,
            dst_ref=wbuf.at[s_from, x_from],
            send_sem=walk_send.at[0, 0],
            recv_sem=walk_recv.at[s_from, x_from],
            device_id=(s_from, L * g + x_from),
            device_id_type=MESH,
        )

    for s_to in range(S):
        for j_to in range(L):
            to_me = s_to * W + j_to * G + lax.div(w, L) == me

            @pl.when(jnp.logical_not(to_me))
            def _():
                walk_copy(s_to, j_to).start()

            @pl.when(to_me)
            def _():
                own = pltpu.make_async_copy(walkers, wbuf.at[s, lax.rem(w, L)], load_sem.at[9])
                own.start()
                own.wait()

    lane = lax.broadcasted_iota(jnp.int32, (1, 128), 1)
    atom = lax.div(lane, 4)
    nuc = []
    for c in range(3):
        along = jnp.zeros((1, 128), F32)
        for a in range(nuclei.shape[1]):
            along = jnp.where(atom == a, nuclei[c : c + 1, a : a + 1], along)
        nuc.append(along)
    kind = lax.rem(lane, 4)
    mine_of = (
        lax.div(lax.broadcasted_iota(jnp.int32, (PAD, 3 * NE), 1), 3)
        == lax.broadcasted_iota(jnp.int32, (PAD, 3 * NE), 0)
    )
    spread = (
        lax.rem(lax.broadcasted_iota(jnp.int32, (3 * NE, 384), 0), 3)
        == lax.div(lax.broadcasted_iota(jnp.int32, (3 * NE, 384), 1), 128)
    )
    spread = jnp.where(spread, 1.0, 0.0).astype(BF16)
    live = lax.broadcasted_iota(jnp.int32, (PAD, 1), 0) < NE

    for s_from in range(S):
        for x_from in range(L):
            from_me = s_from * W + L * g + x_from == me

            @pl.when(jnp.logical_not(from_me))
            def _():
                walk_arrival(s_from, x_from).wait_recv()

    for s_to in range(S):
        for j_to in range(L):
            to_me = s_to * W + j_to * G + lax.div(w, L) == me

            @pl.when(jnp.logical_not(to_me))
            def _():
                walk_copy(s_to, j_to).wait_send()

    for i in range(N):
        for x in range(L):
            row = wbuf[i // L, x, i % L]
            p = i * L + x
            spots[p * PAD : (p + 1) * PAD, :] = jnp.where(mine_of, row, 0.0)

    def features(rows):
        parts = split(spots[rows, :], 3)
        pos = matmul(parts[2], spread) + matmul(parts[1], spread) + matmul(parts[0], spread)
        off = [pos[:, c * 128 : (c + 1) * 128] - nuc[c] for c in range(3)]
        dist = jnp.sqrt(off[0] * off[0] + off[1] * off[1] + off[2] * off[2] + 1.0)
        f = jnp.where(
            kind == 0, off[0], jnp.where(kind == 1, off[1], jnp.where(kind == 2, off[2], dist))
        )
        return jnp.where(lane < FEAT, f, 0.0)

    head_of = lax.div(lax.broadcasted_iota(jnp.int32, (1, D), 1), head_size)
    head_mask = [jnp.where(head_of == h, 1.0, 0.0).astype(F32) for h in range(HEADS)]
    head_mask_bf16 = [mask.astype(BF16) for mask in head_mask]

    def stack_heads(x):
        return jnp.concatenate([x * head_mask_bf16[h] for h in range(HEADS)], axis=0)

    def merge_heads(x):
        return sum(x[h * PAD : (h + 1) * PAD] * head_mask[h] for h in range(HEADS))

    lrow[...] = jnp.zeros_like(lrow)

    def forward(b, carry):
        rows = pl.ds(pl.multiple_of(b * RB, RB), RB)
        f = features(rows)
        feats[rows, :] = f
        h0 = matmul(left(f, 3), s_embed[...])
        normed, scale = normalise(h0)
        x1[rows, :] = normed
        r1[rows, :] = scale
        both = matmul(left(normed, 3), s_qk[...])
        queries, keys = both[:, :D], both[:, D:]
        values = matmul(left(normed, 2), s_w[0])
        q[rows, :] = queries
        k[rows, :] = keys
        v[rows, :] = values
        qs = split(queries, 3)
        ks = split(keys, 3)
        vs = split(values, 2)
        outs = []
        for i in range(WB):
            here = slice(i * PAD, (i + 1) * PAD)
            scores = product(
                [piece[here] for piece in ks], [stack_heads(piece[here]) for piece in qs], NT
            ) / math.sqrt(head_size)
            scores = jnp.where(live, scores, -1e30)
            e = jnp.exp(scores - jnp.max(scores, axis=0, keepdims=True))
            a = e / jnp.sum(e, axis=0, keepdims=True)
            att[b * WB + i] = a
            outs.append(merge_heads(product(split(a.T, 2), [piece[here] for piece in vs], NN)))
        mix = jnp.concatenate(outs, axis=0)
        mixed[rows, :] = mix
        h1 = h0 + matmul(left(mix, 2), s_w[1])
        normed2, scale2 = normalise(h1)
        x2[rows, :] = normed2
        r2[rows, :] = scale2
        t = jnp.tanh(matmul(left(normed2, 2), s_w[2]) + vecs[0:1, :])
        act[rows, :] = t
        last = h1 + t
        h2[rows, :] = last
        out = last * vecs[1:2, :]
        for i in range(WB):
            here = slice(i * PAD, (i + 1) * PAD)
            value = jnp.sum(jnp.where(live, out[here], 0.0)) / NE
            lrow[...] += jnp.where(lane == b * WB + i, value, 0.0)
        return carry

    lax.fori_loop(0, blocks, forward, 0)

    def tab_copy(d):
        other = lax.rem(me + d, S * W)
        return pltpu.make_async_remote_copy(
            src_ref=lrow,
            dst_ref=tab.at[net, g],
            send_sem=tab_send.at[d],
            recv_sem=tab_recv.at[d],
            device_id=(lax.div(other, W), lax.rem(other, W)),
            device_id_type=MESH,
        )

    tab[net, g] = lrow[...]

    def start_tab(d, carry):
        tab_copy(d).start()
        return carry

    lax.fori_loop(1, S * W, start_tab, 0)

    def backward_top(b, carry):
        rows = pl.ds(pl.multiple_of(b * RB, RB), RB)
        gh = vecs[1:2, :] * (1.0 / NE)
        t = act[rows, :]
        dinner = gh * (1.0 - t * t)
        dx2 = matmul(left(dinner, 2), s_t[1])
        act[rows, :] = dinner
        dh1 = gh + normalise_back(dx2, x2[rows, :], r2[rows, :])
        g1[rows, :] = dh1
        dm[rows, :] = matmul(left(dh1, 2), s_t[0])
        return carry

    lax.fori_loop(0, blocks, backward_top, 0)

    def wait_tab(d, carry):
        other = lax.rem(me - d + S * W, S * W)
        wo = lax.rem(other, W)
        from_net = lax.div(other, W) * L + lax.div(wo, G)
        pltpu.make_async_remote_copy(
            src_ref=lrow,
            dst_ref=tab.at[from_net, lax.rem(wo, G)],
            send_sem=tab_send.at[d],
            recv_sem=tab_recv.at[d],
            device_id=(lax.div(other, W), wo),
            device_id_type=MESH,
        ).wait_recv()
        tab_copy(d).wait_send()
        return carry

    lax.fori_loop(1, S * W, wait_tab, 0)

    sub8 = lax.broadcasted_iota(jnp.int32, (N, 128), 0)
    lane8 = lax.broadcasted_iota(jnp.int32, (N, 128), 1)
    state8 = lax.div(lane8, L)
    home8 = jnp.where(state8 == sub8, 1.0, 0.0).astype(F32)
    ident = jnp.where(lane8 == sub8, 1.0, 0.0).astype(F32)

    def ratio_of(logs):
        logs = logs.reshape(N, 128)
        home = jnp.sum(logs * home8, axis=0, keepdims=True)
        return jnp.where(lane8 < held, jnp.exp(logs - home), 0.0)

    summed = ratio_of(tab[:, 0])
    for other in range(1, G):
        summed = summed + ratio_of(tab[:, other])
    coupled = jnp.zeros((N, 128), F32)
    table = jnp.zeros((N, 128), F32)
    for i in range(N):
        col = jnp.sum(jnp.where(state8 == i, summed, 0.0), axis=1, keepdims=True) / total_walkers
        coupled = jnp.where(sub8 == i, jnp.sum(col * home8, axis=0, keepdims=True), coupled)
        table = jnp.where(sub8 == i, jnp.sum(col * ident, axis=0, keepdims=True), table)
    margins[...] = table[:, :N]
    coupled = coupled * (1.0 - home8)
    ratio = ratio_of(tab[:, g])
    terms = coupled * ratio
    denominator = jnp.sum(terms, axis=0, keepdims=True)
    cot = (terms - home8 * denominator) / total_walkers
    cot = jnp.sum(jnp.where(sub8 == net, cot, 0.0), axis=0, keepdims=True)
    rows_of = lax.broadcasted_iota(jnp.int32, (held * PAD, 128), 0)
    first = lax.broadcasted_iota(jnp.int32, (held * PAD, 128), 1) * PAD
    inside = jnp.logical_and(rows_of >= first, rows_of < first + NE)
    ccol[...] = jnp.sum(jnp.where(inside, cot, 0.0), axis=1, keepdims=True)

    outs = [o_weights.at[m] for m in range(5)] + [o_extra]
    results = (f_mlp, f_attn, f_value, f_key, f_query, f_extra)

    def rs_copy(m, d):
        to = lax.rem(g + d, G)
        if m < 5:
            src = part.at[m, pl.ds(pl.multiple_of(to * CH, CH), CH)]
            dst = rbuf.at[m, d - 1]
        else:
            src = part_extra.at[pl.ds(pl.multiple_of(to * EC, EC), EC)]
            dst = rbuf_extra.at[d - 1]
        return pltpu.make_async_remote_copy(
            src_ref=src,
            dst_ref=dst,
            send_sem=rs_send.at[m, d - 1],
            recv_sem=rs_recv.at[m, d - 1],
            device_id=(s, j * G + to),
            device_id_type=MESH,
        )

    def rs_start(m):
        for d in range(1, G):
            rs_copy(m, d).start()

    def piece(m, who):
        jj = lax.div(who, G)
        gg = lax.rem(who, G)
        if m < 5:
            return outs[m].at[jj, 0, pl.ds(pl.multiple_of(gg * CH, CH), CH)]
        return outs[m].at[jj, pl.ds(pl.multiple_of(gg * EC, EC), EC)]

    def rs_finish(m):
        for d in range(1, G):
            rs_copy(m, d).wait_recv()
        if m < 5:
            total = part[m, pl.ds(pl.multiple_of(g * CH, CH), CH)]
            for d in range(1, G):
                total = total + rbuf[m, d - 1]
            outs[m][j, 0, pl.ds(pl.multiple_of(g * CH, CH), CH)] = total
        else:
            total = part_extra[pl.ds(pl.multiple_of(g * EC, EC), EC)]
            for d in range(1, G):
                total = total + rbuf_extra[d - 1]
            outs[m][j, pl.ds(pl.multiple_of(g * EC, EC), EC)] = total

    odd = lax.rem(w, 2)
    place = (1 - odd) * lax.div(w, 2) + odd * (W - lax.div(w + 1, 2))

    def at_place(p):
        p = lax.rem(p + 2 * W, W)
        high = lax.div(p, W // 2)
        return (1 - high) * 2 * p + high * (2 * (W - p) - 1)

    def hops(m, way):
        return W // 2 if (m + way) % 2 == 0 else W - 1 - W // 2

    def ag_copy(m, way, t):
        step = 1 - 2 * way
        block = piece(m, at_place(place - step * t))
        return pltpu.make_async_remote_copy(
            src_ref=block,
            dst_ref=block,
            send_sem=ag_send.at[m, way, t],
            recv_sem=ag_recv.at[m, way, t],
            device_id=(s, at_place(place + step)),
            device_id_type=MESH,
        )

    def ag_arrival(m, way, t):
        step = 1 - 2 * way
        block = piece(m, at_place(place - step * (t + 1)))
        return pltpu.make_async_remote_copy(
            src_ref=block,
            dst_ref=block,
            send_sem=ag_send.at[m, way, t],
            recv_sem=ag_recv.at[m, way, t],
            device_id=(s, at_place(place - step)),
            device_id_type=MESH,
        )

    def ag_step(m, t):
        for way in range(2):
            if 0 < t <= hops(m, way):
                ag_arrival(m, way, t - 1).wait_recv()
            if t < hops(m, way):
                ag_copy(m, way, t).start()
        if t == last:
            flush(m).start()

    last = W // 2

    def flush(m):
        return pltpu.make_async_copy(outs[m], results[m], flush_sem.at[m])

    def ag_finish(m):
        for way in range(2):
            for t in range(hops(m, way)):
                ag_copy(m, way, t).wait_send()
        flush(m).wait()

    todo = [[("sum", 0)] + [("hop", t) for t in range(1, last + 1)] for m in range(6)]

    def advance(*arrays):
        for m in arrays:
            if todo[m]:
                what, t = todo[m].pop(0)
                if what == "sum":
                    rs_finish(m)
                ag_step(m, t)

    c = ccol[...]

    def outer(x, y):
        return matmul(left(x.T, 2), right(y * c, 2))

    part[0] = outer(x2[...], act[...])
    rs_start(0)
    part[1] = outer(mixed[...], g1[...])
    rs_start(1)

    def stacked_gradient(here):
        return [stack_heads(p) for p in split(jnp.where(live, dm[here, :], 0.0), 2)]

    def backward_values(b, carry):
        for i in range(WB):
            here = pl.ds(pl.multiple_of(b * RB + i * PAD, PAD), PAD)
            gv[here, :] = product(split(att[b * WB + i], 2), stacked_gradient(here), NN)
        return carry

    lax.fori_loop(0, blocks, backward_values, 0)
    part[2] = outer(x1[...], gv[...])
    rs_start(2)
    advance(0)
    advance(1)

    def backward_scores(b, carry):
        for i in range(WB):
            here = pl.ds(pl.multiple_of(b * RB + i * PAD, PAD), PAD)
            a = att[b * WB + i]
            ks = split(k[here, :], 2)
            qs = [stack_heads(p) for p in split(q[here, :], 2)]
            da = product(split(v[here, :], 2), stacked_gradient(here), NT)
            ds = a * (da - jnp.sum(a * da, axis=0, keepdims=True)) / math.sqrt(head_size)
            gq[here, :] = merge_heads(product(split(ds.T, 2), ks, NN))
            gk[here, :] = product(split(ds, 2), qs, NN)

        for bb in range(blocks):
            arrays = ((0, 2), (0, 1), (0, 1, 2), (0, 1, 2))[bb % 4] if bb < 4 else ()

            @pl.when(b == bb)
            def _():
                advance(*arrays)

        return carry

    lax.fori_loop(0, blocks, backward_scores, 0)

    x1_left = left(x1[...].T, 2)
    part[3] = matmul(x1_left, right(gk[...] * c, 2))
    rs_start(3)
    part[4] = matmul(x1_left, right(gq[...] * c, 2))
    rs_start(4)
    advance(1, 2)

    def backward_embed(b, carry):
        rows = pl.ds(pl.multiple_of(b * RB, RB), RB)
        dx1 = (
            matmul(left(gq[rows, :], 2), s_qkvt[0])
            + matmul(left(gk[rows, :], 2), s_qkvt[1])
            + matmul(left(gv[rows, :], 2), s_qkvt[2])
        )
        dm[rows, :] = g1[rows, :] + normalise_back(dx1, x1[rows, :], r1[rows, :])
        return carry

    lax.fori_loop(0, blocks, backward_embed, 0)
    advance(3, 4, 2)
    part_extra[...] = jnp.zeros_like(part_extra)
    part_extra[0:FEAT, :] = outer(feats[...], dm[...])[:FEAT]
    part_extra[FEAT : FEAT + 1, :] = jnp.sum(act[...] * c, axis=0, keepdims=True)
    part_extra[FEAT + 1 : FEAT + 2, :] = jnp.sum(h2[...] * c, axis=0, keepdims=True) / NE
    rs_start(5)
    advance(3, 4)
    while any(todo):
        advance(*range(6))
    for m in range(6):
        ag_finish(m)
        for d in range(1, G):
            rs_copy(m, d).wait_send()


def finish_kernel(
    m_in, mlp, attn, value, key, query, extra,
    margins, o_embed, o_query, o_key, o_value, o_attn, o_mlp, o_bias, o_out, held, sem,
):
    feat = o_embed.shape[1]
    margins[...] = m_in[...]
    pairs = ((query, o_query), (key, o_key), (value, o_value), (attn, o_attn), (mlp, o_mlp))
    ins = [pltpu.make_async_copy(src, held.at[n], sem.at[n]) for n, (src, _) in enumerate(pairs)]
    copies = [
        pltpu.make_async_copy(held.at[n], dst, sem.at[5 + n]) for n, (_, dst) in enumerate(pairs)
    ]
    for copy in ins:
        copy.start()
    for n in range(5):
        ins[n].wait()
        copies[n].start()
    for n in range(o_embed.shape[0]):
        o_embed[n] = extra[n, :feat]
        o_bias[n] = extra[n, feat : feat + 1]
        o_out[n : n + 1, :] = extra[n, feat + 1 : feat + 2]
    for copy in copies:
        copy.wait()


def shards(walkers, nuclei, w_embed, w_query, w_key, w_value, w_attn_out, w_mlp, b_mlp, w_out):
    S = lax.axis_size("state")
    W = lax.axis_size("walker")
    L, per_device, coords = walkers.shape
    assert per_device == 1 and W % (2 * L) == 0
    G = W // L
    N = S * L
    NE = coords // 3
    PAD = -(-NE // 16) * 16
    FEAT, D = w_embed.shape[1:]
    CH = D // G
    rows_extra = max(-(-(FEAT + 2) // (8 * G)) * 8 * G, 8 * G)
    EC = rows_extra // G
    held = N * L
    R = held * PAD
    cfg = (S, W, L, G, N, NE, PAD, D, FEAT, CH, EC)
    vmem = pl.BlockSpec(memory_space=pltpu.VMEM)
    hbm = pl.BlockSpec(memory_space=pl.ANY)
    full = lambda: pltpu.VMEM((R, D), F32)
    column = lambda: pltpu.VMEM((R, 1), F32)
    weight = jax.ShapeDtypeStruct((L, 1, D, D), F32)
    dma = pltpu.SemaphoreType.DMA
    outs = pl.pallas_call(
        functools.partial(kernel, cfg),
        out_shape=(
            jax.ShapeDtypeStruct((N, N), F32),
            weight, weight, weight, weight, weight,
            jax.ShapeDtypeStruct((L, rows_extra, D), F32),
        ),
        in_specs=[hbm] * 10,
        out_specs=(vmem,) + (hbm,) * 6,
        scratch_shapes=[
            pltpu.VMEM((5, L, 1, D, D), F32),
            pltpu.VMEM((L, rows_extra, D), F32),
            pltpu.VMEM(nuclei.shape[::-1], F32),
            pltpu.VMEM(b_mlp.shape, F32),
            pltpu.VMEM(w_out.shape, F32),
            pltpu.VMEM((S, L, L, 1, coords), F32),
            pltpu.VMEM((128, D), F32),
            pltpu.VMEM((5, D, D), F32),
            pltpu.VMEM((8, D), F32),
            pltpu.VMEM((6 * 128, D), BF16),
            pltpu.VMEM((6 * D, 2 * D), BF16),
            pltpu.VMEM((3, 3 * D, D), BF16),
            pltpu.VMEM((3, 3 * D, D), BF16),
            pltpu.VMEM((2, 3 * D, D), BF16),
            pltpu.VMEM((R, coords), F32),
            pltpu.VMEM((R, 128), F32),
            full(), column(), full(), full(), full(),
            pltpu.VMEM((held, PAD, HEADS * PAD), F32),
            full(), full(), column(), full(), full(),
            full(), full(), full(), full(), full(),
            pltpu.VMEM((1, 128), F32),
            pltpu.VMEM((N, G, 1, 128), F32),
            pltpu.VMEM((5, D, D), F32),
            pltpu.VMEM((rows_extra, D), F32),
            pltpu.VMEM((5, G - 1, CH, D), F32),
            pltpu.VMEM((G - 1, EC, D), F32),
            column(),
            dma((10,)), dma((6,)),
            dma((S, L)), dma((S, L)),
            dma((S * W,)), dma((S * W,)),
            dma((6, G - 1)), dma((6, G - 1)),
            dma((6, 2, W // 2)), dma((6, 2, W // 2)),
        ],
        compiler_params=pltpu.CompilerParams(
            collective_id=0, has_side_effects=True, vmem_limit_bytes=56 * 1024 * 1024
        ),
    )(walkers, nuclei.T, w_embed, w_query, w_key, w_value, w_attn_out, w_mlp, b_mlp, w_out)
    like = lambda x: jax.ShapeDtypeStruct(x.shape, F32)
    return pl.pallas_call(
        finish_kernel,
        out_shape=(
            jax.ShapeDtypeStruct((N, N), F32),
            like(w_embed), weight, weight, weight, weight, weight, like(b_mlp), like(w_out),
        ),
        in_specs=[vmem] + [hbm] * 5 + [vmem],
        out_specs=(vmem, vmem) + (hbm,) * 5 + (vmem, vmem),
        scratch_shapes=[pltpu.VMEM((5, L, 1, D, D), F32), dma((10,))],
        compiler_params=pltpu.CompilerParams(vmem_limit_bytes=56 * 1024 * 1024),
    )(*outs)


def solution(mesh):
    return jax.shard_map(
        shards,
        mesh=mesh,
        in_specs=(
            P("state", "walker", None),
            P(),
            P("state", None, None),
            P("state", None, None, None),
            P("state", None, None, None),
            P("state", None, None, None),
            P("state", None, None, None),
            P("state", None, None, None),
            P("state", None, None),
            P("state", None),
        ),
        out_specs=(
            P(),
            P("state", None, None),
            P("state", None, None, None),
            P("state", None, None, None),
            P("state", None, None, None),
            P("state", None, None, None),
            P("state", None, None, None),
            P("state", None, None),
            P("state", None),
        ),
        check_vma=False,
    )
```

```python
import functools
import math

import jax
import jax.numpy as jnp
from jax import lax
from jax.experimental import pallas as pl
from jax.experimental.pallas import tpu as pltpu
from jax.sharding import PartitionSpec as P

HEADS = 4
EPS = 1e-05
F32 = jnp.float32
BF16 = jnp.bfloat16
MESH = pl.DeviceIdType.MESH
WALKERS_PER_BLOCK = 8

NN = (((1,), (0,)), ((), ()))
NT = (((1,), (1,)), ((), ()))
TN = (((0,), (0,)), ((), ()))


def split(x, parts):
    out = []
    for part in range(parts):
        piece = x.astype(BF16)
        out.append(piece)
        if part + 1 < parts:
            x = x - piece.astype(F32)
    return out


def terms(parts):
    return [(i, order - i) for order in range(parts - 1, -1, -1) for i in range(order + 1)]


def left(x, parts):
    pieces = split(x, parts)
    return jnp.concatenate([pieces[i] for i, _ in terms(parts)], axis=1)


def right(x, parts):
    pieces = split(x, parts)
    return jnp.concatenate([pieces[i] for _, i in terms(parts)], axis=0)


def matmul(a, b, dims=NN):
    return lax.dot_general(a, b, dims, preferred_element_type=F32)


def product(a, b, dims):
    parts, rows = len(a), a[0].shape[0]
    sums = [None] * parts
    for n in range(parts - 1, -1, -1):
        tall = matmul(jnp.concatenate(a[: parts - n], axis=0), b[n], dims)
        for i in range(parts - n):
            term = tall[i * rows : (i + 1) * rows]
            sums[i + n] = term if sums[i + n] is None else sums[i + n] + term
    total = sums[-1]
    for term in sums[-2::-1]:
        total = total + term
    return total


def normalise(hidden):
    centre = hidden - jnp.mean(hidden, axis=-1, keepdims=True)
    spread = jnp.mean(centre * centre, axis=-1, keepdims=True)
    scale = 1.0 / jnp.sqrt(spread + EPS)
    return centre * scale, scale


def normalise_back(grad, normed, scale):
    mean = jnp.mean(grad, axis=-1, keepdims=True)
    along = jnp.mean(grad * normed, axis=-1, keepdims=True)
    return scale * (grad - mean - normed * along)


def kernel(
    cfg,
    walkers, nuclei_in, w_embed, w_query, w_key, w_value, w_attn, w_mlp, b_mlp_in, w_out_in,
    margins, f_mlp, f_attn, f_value, f_key, f_query, f_extra,
    o_weights, o_extra, nuclei, b_mlp, w_out, wbuf, raw_embed, raw, vecs, s_embed, s_qk, s_w, s_qkvt, s_t, spots, feats, x1, r1, q, k, v, att, mixed, x2, r2, act, h2,
    g1, gk, gq, gv, dm, lrow, tab, part, part_extra, rbuf, rbuf_extra, ccol,
    load_sem, flush_sem, walk_send, walk_recv, tab_send, tab_recv, rs_send, rs_recv, ag_send, ag_recv,
):
    S, W, L, G, N, NE, PAD, D, FEAT, CH, EC = cfg
    held = N * L
    head_size = D // HEADS
    WB = WALKERS_PER_BLOCK
    RB = WB * PAD
    blocks = held // WB
    total_walkers = W
    s = lax.axis_index("state")
    w = lax.axis_index("walker")
    j = lax.div(w, G)
    g = lax.rem(w, G)
    net = s * L + j
    me = s * W + w

    loads = [pltpu.make_async_copy(w_embed.at[j], raw_embed.at[pl.ds(0, FEAT)], load_sem.at[0])]
    for n, ref in enumerate((w_query, w_key, w_value, w_attn, w_mlp)):
        loads.append(pltpu.make_async_copy(ref.at[j, 0], raw.at[n], load_sem.at[1 + n]))
    for n, (src, dst) in enumerate(((nuclei_in, nuclei), (b_mlp_in, b_mlp), (w_out_in, w_out))):
        loads.append(pltpu.make_async_copy(src, dst, load_sem.at[6 + n]))
    for copy in loads:
        copy.start()

    barrier = pltpu.get_barrier_semaphore()

    def greet(d, carry):
        other = lax.rem(me + d, S * W)
        pl.semaphore_signal(
            barrier, inc=1, device_id=(lax.div(other, W), lax.rem(other, W)), device_id_type=MESH
        )
        return carry

    lax.fori_loop(1, S * W, greet, 0)

    raw_embed[FEAT:, :] = jnp.zeros((128 - FEAT, D), F32)
    for copy in loads:
        copy.wait()
    s_embed[...] = right(raw_embed[...], 3)
    s_qk[...] = jnp.concatenate([right(raw[0], 3), right(raw[1], 3)], axis=1)
    for n in range(3):
        s_w[n] = right(raw[2 + n], 2)
        s_qkvt[n] = right(raw[n].T, 2)
    for n in range(2):
        s_t[n] = right(raw[3 + n].T, 2)
    vecs[0:1, :] = b_mlp[j]
    vecs[1:2, :] = w_out[pl.ds(j, 1), :]

    pl.semaphore_wait(barrier, S * W - 1)

    def walk_copy(s_to, j_to):
        return pltpu.make_async_remote_copy(
            src_ref=walkers,
            dst_ref=wbuf.at[s, lax.rem(w, L)],
            send_sem=walk_send.at[s_to, j_to],
            recv_sem=walk_recv.at[s, lax.rem(w, L)],
            device_id=(s_to, j_to * G + lax.div(w, L)),
            device_id_type=MESH,
        )

    def walk_arrival(s_from, x_from):
        return pltpu.make_async_remote_copy(
            src_ref=walkers,
            dst_ref=wbuf.at[s_from, x_from],
            send_sem=walk_send.at[0, 0],
            recv_sem=walk_recv.at[s_from, x_from],
            device_id=(s_from, L * g + x_from),
            device_id_type=MESH,
        )

    for s_to in range(S):
        for j_to in range(L):
            to_me = s_to * W + j_to * G + lax.div(w, L) == me

            @pl.when(jnp.logical_not(to_me))
            def _():
                walk_copy(s_to, j_to).start()

            @pl.when(to_me)
            def _():
                own = pltpu.make_async_copy(walkers, wbuf.at[s, lax.rem(w, L)], load_sem.at[9])
                own.start()
                own.wait()

    lane = lax.broadcasted_iota(jnp.int32, (1, 128), 1)
    atom = lax.div(lane, 4)
    nuc = []
    for c in range(3):
        along = jnp.zeros((1, 128), F32)
        for a in range(nuclei.shape[1]):
            along = jnp.where(atom == a, nuclei[c : c + 1, a : a + 1], along)
        nuc.append(along)
    kind = lax.rem(lane, 4)
    mine_of = (
        lax.div(lax.broadcasted_iota(jnp.int32, (PAD, 3 * NE), 1), 3)
        == lax.broadcasted_iota(jnp.int32, (PAD, 3 * NE), 0)
    )
    spread = (
        lax.rem(lax.broadcasted_iota(jnp.int32, (3 * NE, 384), 0), 3)
        == lax.div(lax.broadcasted_iota(jnp.int32, (3 * NE, 384), 1), 128)
    )
    spread = jnp.where(spread, 1.0, 0.0).astype(BF16)
    live = lax.broadcasted_iota(jnp.int32, (PAD, 1), 0) < NE

    for s_from in range(S):
        for x_from in range(L):
            from_me = s_from * W + L * g + x_from == me

            @pl.when(jnp.logical_not(from_me))
            def _():
                walk_arrival(s_from, x_from).wait_recv()

    for s_to in range(S):
        for j_to in range(L):
            to_me = s_to * W + j_to * G + lax.div(w, L) == me

            @pl.when(jnp.logical_not(to_me))
            def _():
                walk_copy(s_to, j_to).wait_send()

    for i in range(N):
        for x in range(L):
            row = wbuf[i // L, x, i % L]
            p = i * L + x
            spots[p * PAD : (p + 1) * PAD, :] = jnp.where(mine_of, row, 0.0)

    def features(rows):
        parts = split(spots[rows, :], 3)
        pos = matmul(parts[2], spread) + matmul(parts[1], spread) + matmul(parts[0], spread)
        off = [pos[:, c * 128 : (c + 1) * 128] - nuc[c] for c in range(3)]
        dist = jnp.sqrt(off[0] * off[0] + off[1] * off[1] + off[2] * off[2] + 1.0)
        f = jnp.where(
            kind == 0, off[0], jnp.where(kind == 1, off[1], jnp.where(kind == 2, off[2], dist))
        )
        return jnp.where(lane < FEAT, f, 0.0)

    head_of = lax.div(lax.broadcasted_iota(jnp.int32, (1, D), 1), head_size)
    head_mask = [jnp.where(head_of == h, 1.0, 0.0).astype(F32) for h in range(HEADS)]
    head_mask_bf16 = [mask.astype(BF16) for mask in head_mask]

    def stack_heads(x):
        return jnp.concatenate([x * head_mask_bf16[h] for h in range(HEADS)], axis=0)

    def merge_heads(x):
        return sum(x[h * PAD : (h + 1) * PAD] * head_mask[h] for h in range(HEADS))

    lrow[...] = jnp.zeros_like(lrow)

    def forward(b, carry):
        rows = pl.ds(pl.multiple_of(b * RB, RB), RB)
        f = features(rows)
        feats[rows, :] = f
        h0 = matmul(left(f, 3), s_embed[...])
        normed, scale = normalise(h0)
        x1[rows, :] = normed
        r1[rows, :] = scale
        both = matmul(left(normed, 3), s_qk[...])
        queries, keys = both[:, :D], both[:, D:]
        values = matmul(left(normed, 2), s_w[0])
        q[rows, :] = queries
        k[rows, :] = keys
        v[rows, :] = values
        qs = split(queries, 3)
        ks = split(keys, 3)
        vs = split(values, 2)
        outs = []
        for i in range(WB):
            here = slice(i * PAD, (i + 1) * PAD)
            scores = product(
                [piece[here] for piece in ks], [stack_heads(piece[here]) for piece in qs], NT
            ) / math.sqrt(head_size)
            scores = jnp.where(live, scores, -1e30)
            e = jnp.exp(scores - jnp.max(scores, axis=0, keepdims=True))
            a = e / jnp.sum(e, axis=0, keepdims=True)
            att[b * WB + i] = a
            outs.append(merge_heads(product(split(a.T, 2), [piece[here] for piece in vs], NN)))
        mix = jnp.concatenate(outs, axis=0)
        mixed[rows, :] = mix
        h1 = h0 + matmul(left(mix, 2), s_w[1])
        normed2, scale2 = normalise(h1)
        x2[rows, :] = normed2
        r2[rows, :] = scale2
        t = jnp.tanh(matmul(left(normed2, 2), s_w[2]) + vecs[0:1, :])
        act[rows, :] = t
        last = h1 + t
        h2[rows, :] = last
        out = last * vecs[1:2, :]
        for i in range(WB):
            here = slice(i * PAD, (i + 1) * PAD)
            value = jnp.sum(jnp.where(live, out[here], 0.0)) / NE
            lrow[...] += jnp.where(lane == b * WB + i, value, 0.0)
        return carry

    lax.fori_loop(0, blocks, forward, 0)

    def tab_copy(d):
        other = lax.rem(me + d, S * W)
        return pltpu.make_async_remote_copy(
            src_ref=lrow,
            dst_ref=tab.at[net, g],
            send_sem=tab_send.at[d],
            recv_sem=tab_recv.at[d],
            device_id=(lax.div(other, W), lax.rem(other, W)),
            device_id_type=MESH,
        )

    tab[net, g] = lrow[...]

    def start_tab(d, carry):
        tab_copy(d).start()
        return carry

    lax.fori_loop(1, S * W, start_tab, 0)

    def backward_top(b, carry):
        rows = pl.ds(pl.multiple_of(b * RB, RB), RB)
        gh = vecs[1:2, :] * (1.0 / NE)
        t = act[rows, :]
        dinner = gh * (1.0 - t * t)
        dx2 = matmul(left(dinner, 2), s_t[1])
        act[rows, :] = dinner
        dh1 = gh + normalise_back(dx2, x2[rows, :], r2[rows, :])
        g1[rows, :] = dh1
        dm[rows, :] = matmul(left(dh1, 2), s_t[0])
        return carry

    lax.fori_loop(0, blocks, backward_top, 0)

    def wait_tab(d, carry):
        other = lax.rem(me - d + S * W, S * W)
        wo = lax.rem(other, W)
        from_net = lax.div(other, W) * L + lax.div(wo, G)
        pltpu.make_async_remote_copy(
            src_ref=lrow,
            dst_ref=tab.at[from_net, lax.rem(wo, G)],
            send_sem=tab_send.at[d],
            recv_sem=tab_recv.at[d],
            device_id=(lax.div(other, W), wo),
            device_id_type=MESH,
        ).wait_recv()
        tab_copy(d).wait_send()
        return carry

    lax.fori_loop(1, S * W, wait_tab, 0)

    sub8 = lax.broadcasted_iota(jnp.int32, (N, 128), 0)
    lane8 = lax.broadcasted_iota(jnp.int32, (N, 128), 1)
    state8 = lax.div(lane8, L)
    home8 = jnp.where(state8 == sub8, 1.0, 0.0).astype(F32)
    ident = jnp.where(lane8 == sub8, 1.0, 0.0).astype(F32)

    def ratio_of(logs):
        logs = logs.reshape(N, 128)
        home = jnp.sum(logs * home8, axis=0, keepdims=True)
        return jnp.where(lane8 < held, jnp.exp(logs - home), 0.0)

    summed = ratio_of(tab[:, 0])
    for other in range(1, G):
        summed = summed + ratio_of(tab[:, other])
    coupled = jnp.zeros((N, 128), F32)
    table = jnp.zeros((N, 128), F32)
    for i in range(N):
        col = jnp.sum(jnp.where(state8 == i, summed, 0.0), axis=1, keepdims=True) / total_walkers
        coupled = jnp.where(sub8 == i, jnp.sum(col * home8, axis=0, keepdims=True), coupled)
        table = jnp.where(sub8 == i, jnp.sum(col * ident, axis=0, keepdims=True), table)
    margins[...] = table[:, :N]
    coupled = coupled * (1.0 - home8)
    ratio = ratio_of(tab[:, g])
    terms = coupled * ratio
    denominator = jnp.sum(terms, axis=0, keepdims=True)
    cot = (terms - home8 * denominator) / total_walkers
    cot = jnp.sum(jnp.where(sub8 == net, cot, 0.0), axis=0, keepdims=True)
    rows_of = lax.broadcasted_iota(jnp.int32, (held * PAD, 128), 0)
    first = lax.broadcasted_iota(jnp.int32, (held * PAD, 128), 1) * PAD
    inside = jnp.logical_and(rows_of >= first, rows_of < first + NE)
    ccol[...] = jnp.sum(jnp.where(inside, cot, 0.0), axis=1, keepdims=True)

    outs = [o_weights.at[m] for m in range(5)] + [o_extra]
    results = (f_mlp, f_attn, f_value, f_key, f_query, f_extra)

    bits = G.bit_length() - 1
    own_bit = [lax.rem(lax.div(g, 1 << i), 2) for i in range(bits)]

    def rs_rows(m, block):
        if m < 5:
            return part.at[m, pl.ds(pl.multiple_of(block * CH, CH), CH)]
        return part_extra.at[pl.ds(pl.multiple_of(block * EC, EC), EC)]

    def rs_slot(m, n):
        return rbuf.at[m, n] if m < 5 else rbuf_extra.at[n]

    def rs_stage(m, stage):
        order = range(bits) if m % 2 else range(bits - 1, -1, -1)
        order = list(order)
        bit, rest = order[stage], order[stage + 1 :]
        fixed = sum((own_bit[i] * (1 << i) for i in order[:stage]), 0)
        first = sum(G >> (i + 1) for i in range(stage))
        partner = g + (1 - 2 * own_bit[bit]) * (1 << bit)
        copies, kept = [], []
        for n in range(1 << len(rest)):
            free = sum(((n >> i) & 1) << place for i, place in enumerate(rest))
            sent = fixed + (1 - own_bit[bit]) * (1 << bit) + free
            kept.append((first + n, fixed + own_bit[bit] * (1 << bit) + free))
            copies.append(
                pltpu.make_async_remote_copy(
                    src_ref=rs_rows(m, sent),
                    dst_ref=rs_slot(m, first + n),
                    send_sem=rs_send.at[m, first + n],
                    recv_sem=rs_recv.at[m, first + n],
                    device_id=(s, j * G + partner),
                    device_id_type=MESH,
                )
            )
        return copies, kept

    def rs_start(m, stage=0):
        for copy in rs_stage(m, stage)[0]:
            copy.start()

    def rs_add(m, stage):
        copies, kept = rs_stage(m, stage)
        for copy, (n, block) in zip(copies, kept):
            copy.wait_recv()
            rows = rs_rows(m, block)
            rows[...] = rows[...] + rs_slot(m, n)[...]

    def rs_finish(m):
        rs_add(m, bits - 1)
        piece(m, w)[...] = rs_rows(m, g)[...]

    def piece(m, who):
        jj = lax.div(who, G)
        gg = lax.rem(who, G)
        if m < 5:
            return outs[m].at[jj, 0, pl.ds(pl.multiple_of(gg * CH, CH), CH)]
        return outs[m].at[jj, pl.ds(pl.multiple_of(gg * EC, EC), EC)]

    odd = lax.rem(w, 2)
    place = (1 - odd) * lax.div(w, 2) + odd * (W - lax.div(w + 1, 2))

    def at_place(p):
        p = lax.rem(p + 2 * W, W)
        high = lax.div(p, W // 2)
        return (1 - high) * 2 * p + high * (2 * (W - p) - 1)

    def hops(m, way):
        return W // 2 if (m + way) % 2 == 0 else W - 1 - W // 2

    def ag_copy(m, way, t):
        step = 1 - 2 * way
        block = piece(m, at_place(place - step * t))
        return pltpu.make_async_remote_copy(
            src_ref=block,
            dst_ref=block,
            send_sem=ag_send.at[m, way, t],
            recv_sem=ag_recv.at[m, way, t],
            device_id=(s, at_place(place + step)),
            device_id_type=MESH,
        )

    def ag_arrival(m, way, t):
        step = 1 - 2 * way
        block = piece(m, at_place(place - step * (t + 1)))
        return pltpu.make_async_remote_copy(
            src_ref=block,
            dst_ref=block,
            send_sem=ag_send.at[m, way, t],
            recv_sem=ag_recv.at[m, way, t],
            device_id=(s, at_place(place - step)),
            device_id_type=MESH,
        )

    def ag_step(m, t):
        for way in range(2):
            if 0 < t <= hops(m, way):
                ag_arrival(m, way, t - 1).wait_recv()
            if t < hops(m, way):
                ag_copy(m, way, t).start()
        if t == last:
            flush(m).start()

    last = W // 2

    def flush(m):
        return pltpu.make_async_copy(outs[m], results[m], flush_sem.at[m])

    def ag_finish(m):
        for way in range(2):
            for t in range(hops(m, way)):
                ag_copy(m, way, t).wait_send()
        flush(m).wait()

    todo = [[("half", n) for n in range(bits - 1)] + [("sum", 0)] + [("hop", t) for t in range(1, last + 1)] for m in range(6)]

    def take(*arrays):
        return [(m,) + todo[m].pop(0) for m in arrays if todo[m]]

    def act_on(steps):
        for m, what, t in steps:
            if what == "half":
                rs_add(m, t)
                rs_start(m, t + 1)
                continue
            if what == "sum":
                rs_finish(m)
            ag_step(m, t)

    def advance(*arrays):
        act_on(take(*arrays))

    def at(plan, b, i):
        for (block, place), steps in plan.items():
            if place == i:

                @pl.when(b == block)
                def _():
                    act_on(steps)

    c = ccol[...]

    def outer(x, y):
        return matmul(left(x.T, 2), right(y * c, 2))

    part[0] = outer(x2[...], act[...])
    rs_start(0)
    part[1] = outer(mixed[...], g1[...])
    rs_start(1)

    def stacked_gradient(here):
        return [stack_heads(p) for p in split(jnp.where(live, dm[here, :], 0.0), 2)]

    def backward_values(b, carry):
        for i in range(WB):
            here = pl.ds(pl.multiple_of(b * RB + i * PAD, PAD), PAD)
            gv[here, :] = product(split(att[b * WB + i], 2), stacked_gradient(here), NN)
        at(value_plan, b, 0)
        return carry

    value_plan = {(0, 0): take(0), (1, 0): take(0, 1)}
    lax.fori_loop(0, blocks, backward_values, 0)
    part[2] = outer(x1[...], gv[...])
    rs_start(2)
    advance(0, 1)

    def backward_scores(b, carry):
        for i in range(WB):
            here = pl.ds(pl.multiple_of(b * RB + i * PAD, PAD), PAD)
            a = att[b * WB + i]
            ks = split(k[here, :], 2)
            qs = [stack_heads(p) for p in split(q[here, :], 2)]
            da = product(split(v[here, :], 2), stacked_gradient(here), NT)
            ds = a * (da - jnp.sum(a * da, axis=0, keepdims=True)) / math.sqrt(head_size)
            gq[here, :] = merge_heads(product(split(ds.T, 2), ks, NN))
            gk[here, :] = product(split(ds, 2), qs, NN)
            at(score_plan, b, i)

        return carry

    score_plan = {
        (0, 1): take(0), (0, 3): take(1, 2), (0, 5): take(0, 2), (0, 7): take(1),
        (1, 1): take(0, 2), (1, 3): take(1, 2), (1, 5): take(1), (1, 7): take(2),
    }
    lax.fori_loop(0, blocks, backward_scores, 0)

    x1_left = left(x1[...].T, 2)
    part[3] = matmul(x1_left, right(gk[...] * c, 2))
    rs_start(3)
    advance(2)
    part[4] = matmul(x1_left, right(gq[...] * c, 2))
    rs_start(4)
    advance(3)

    def backward_embed(b, carry):
        rows = pl.ds(pl.multiple_of(b * RB, RB), RB)
        dx1 = (
            matmul(left(gq[rows, :], 2), s_qkvt[0])
            + matmul(left(gk[rows, :], 2), s_qkvt[1])
            + matmul(left(gv[rows, :], 2), s_qkvt[2])
        )
        dm[rows, :] = g1[rows, :] + normalise_back(dx1, x1[rows, :], r1[rows, :])
        at(embed_plan, b, 0)
        return carry

    embed_plan = {(0, 0): take(3, 4), (1, 0): take(3, 4)}
    lax.fori_loop(0, blocks, backward_embed, 0)
    part_extra[...] = jnp.zeros_like(part_extra)
    part_extra[0:FEAT, :] = outer(feats[...], dm[...])[:FEAT]
    part_extra[FEAT : FEAT + 1, :] = jnp.sum(act[...] * c, axis=0, keepdims=True)
    part_extra[FEAT + 1 : FEAT + 2, :] = jnp.sum(h2[...] * c, axis=0, keepdims=True) / NE
    rs_start(5)
    advance(3, 4)
    while any(todo):
        advance(*range(6))
    for m in range(6):
        ag_finish(m)
        for stage in range(bits):
            for copy in rs_stage(m, stage)[0]:
                copy.wait_send()


def finish_kernel(
    m_in, mlp, attn, value, key, query, extra,
    margins, o_embed, o_query, o_key, o_value, o_attn, o_mlp, o_bias, o_out, held, sem,
):
    feat = o_embed.shape[1]
    margins[...] = m_in[...]
    pairs = ((query, o_query), (key, o_key), (value, o_value), (attn, o_attn), (mlp, o_mlp))
    L = o_embed.shape[0]
    places = [(n, i) for n in range(5) for i in range(L)]
    ins = [
        pltpu.make_async_copy(pairs[n][0].at[i], held.at[n, i], sem.at[0, n, i]) for n, i in places
    ]
    copies = [
        pltpu.make_async_copy(held.at[n, i], pairs[n][1].at[i], sem.at[1, n, i]) for n, i in places
    ]
    for copy in ins:
        copy.start()
    for n in range(len(places)):
        ins[n].wait()
        copies[n].start()
    for n in range(o_embed.shape[0]):
        o_embed[n] = extra[n, :feat]
        o_bias[n] = extra[n, feat : feat + 1]
        o_out[n : n + 1, :] = extra[n, feat + 1 : feat + 2]
    for copy in copies:
        copy.wait()


def shards(walkers, nuclei, w_embed, w_query, w_key, w_value, w_attn_out, w_mlp, b_mlp, w_out):
    S = lax.axis_size("state")
    W = lax.axis_size("walker")
    L, per_device, coords = walkers.shape
    assert per_device == 1 and W % (2 * L) == 0
    G = W // L
    N = S * L
    NE = coords // 3
    PAD = -(-NE // 16) * 16
    FEAT, D = w_embed.shape[1:]
    CH = D // G
    rows_extra = max(-(-(FEAT + 2) // (8 * G)) * 8 * G, 8 * G)
    EC = rows_extra // G
    held = N * L
    R = held * PAD
    cfg = (S, W, L, G, N, NE, PAD, D, FEAT, CH, EC)
    vmem = pl.BlockSpec(memory_space=pltpu.VMEM)
    hbm = pl.BlockSpec(memory_space=pl.ANY)
    full = lambda: pltpu.VMEM((R, D), F32)
    column = lambda: pltpu.VMEM((R, 1), F32)
    weight = jax.ShapeDtypeStruct((L, 1, D, D), F32)
    dma = pltpu.SemaphoreType.DMA
    outs = pl.pallas_call(
        functools.partial(kernel, cfg),
        out_shape=(
            jax.ShapeDtypeStruct((N, N), F32),
            weight, weight, weight, weight, weight,
            jax.ShapeDtypeStruct((L, rows_extra, D), F32),
        ),
        in_specs=[hbm] * 10,
        out_specs=(vmem,) + (hbm,) * 6,
        scratch_shapes=[
            pltpu.VMEM((5, L, 1, D, D), F32),
            pltpu.VMEM((L, rows_extra, D), F32),
            pltpu.VMEM(nuclei.shape[::-1], F32),
            pltpu.VMEM(b_mlp.shape, F32),
            pltpu.VMEM(w_out.shape, F32),
            pltpu.VMEM((S, L, L, 1, coords), F32),
            pltpu.VMEM((128, D), F32),
            pltpu.VMEM((5, D, D), F32),
            pltpu.VMEM((8, D), F32),
            pltpu.VMEM((6 * 128, D), BF16),
            pltpu.VMEM((6 * D, 2 * D), BF16),
            pltpu.VMEM((3, 3 * D, D), BF16),
            pltpu.VMEM((3, 3 * D, D), BF16),
            pltpu.VMEM((2, 3 * D, D), BF16),
            pltpu.VMEM((R, coords), F32),
            pltpu.VMEM((R, 128), F32),
            full(), column(), full(), full(), full(),
            pltpu.VMEM((held, PAD, HEADS * PAD), F32),
            full(), full(), column(), full(), full(),
            full(), full(), full(), full(), full(),
            pltpu.VMEM((1, 128), F32),
            pltpu.VMEM((N, G, 1, 128), F32),
            pltpu.VMEM((5, D, D), F32),
            pltpu.VMEM((rows_extra, D), F32),
            pltpu.VMEM((5, G - 1, CH, D), F32),
            pltpu.VMEM((G - 1, EC, D), F32),
            column(),
            dma((10,)), dma((6,)),
            dma((S, L)), dma((S, L)),
            dma((S * W,)), dma((S * W,)),
            dma((6, G - 1)), dma((6, G - 1)),
            dma((6, 2, W // 2)), dma((6, 2, W // 2)),
        ],
        compiler_params=pltpu.CompilerParams(
            collective_id=0, has_side_effects=True, vmem_limit_bytes=56 * 1024 * 1024
        ),
    )(walkers, nuclei.T, w_embed, w_query, w_key, w_value, w_attn_out, w_mlp, b_mlp, w_out)
    like = lambda x: jax.ShapeDtypeStruct(x.shape, F32)
    return pl.pallas_call(
        finish_kernel,
        out_shape=(
            jax.ShapeDtypeStruct((N, N), F32),
            like(w_embed), weight, weight, weight, weight, weight, like(b_mlp), like(w_out),
        ),
        in_specs=[vmem] + [hbm] * 5 + [vmem],
        out_specs=(vmem, vmem) + (hbm,) * 5 + (vmem, vmem),
        scratch_shapes=[pltpu.VMEM((5, L, 1, D, D), F32), dma((2, 5, L))],
        compiler_params=pltpu.CompilerParams(vmem_limit_bytes=56 * 1024 * 1024),
    )(*outs)


def solution(mesh):
    return jax.shard_map(
        shards,
        mesh=mesh,
        in_specs=(
            P("state", "walker", None),
            P(),
            P("state", None, None),
            P("state", None, None, None),
            P("state", None, None, None),
            P("state", None, None, None),
            P("state", None, None, None),
            P("state", None, None, None),
            P("state", None, None),
            P("state", None),
        ),
        out_specs=(
            P(),
            P("state", None, None),
            P("state", None, None, None),
            P("state", None, None, None),
            P("state", None, None, None),
            P("state", None, None, None),
            P("state", None, None, None),
            P("state", None, None),
            P("state", None),
        ),
        check_vma=False,
    )
```
